128 devices in a mesh: dp: 8 (over z, core), expert: 16 (over y, x).
Axes of the slice: x: 4, y: 4, z: 4, core: 2. Of those that a mesh axis runs over, the one named last changes fastest.
Arguments:
- tokens: bfloat16 [16384, 2048], P(('dp', 'expert')), may hold values from -24 to 24
- expert_ids: int32 [16384, 6], P(('dp', 'expert')), may hold values from 0 to 31, all different within a row; in each aligned block of 128 rows (0 to 127, 128 to 255, ...) at most 32 rows name the same one
- combine_weight: float32 [16384, 6], P(('dp', 'expert')), may hold values from 0.05 to 1
- partner: int32 [16], replicated, may hold values from 0 to 15, as said below
- w_up: bfloat16 [2048, 32, 768], P(None, 'expert'), may hold values from -0.125 to 0.125
- w_down: bfloat16 [2048, 32, 768], P(None, 'expert'), may hold values from -0.21875 to 0.21875
- out_grad: bfloat16 [16384, 2048], P(('dp', 'expert')), may hold values from -6 to 6
Outputs:
- output: bfloat16 [16384, 2048], P(('dp', 'expert'))
- input_grad: bfloat16 [16384, 2048], P(('dp', 'expert'))
- grad_up: bfloat16 [2048, 32, 768], P('dp', 'expert')
- grad_down: bfloat16 [2048, 32, 768], P('dp', 'expert')
The draws below stay inside these ranges and needn't reach their ends.
Inputs may be any that keep to these rules, and one draw needn't show every extreme that they name: `expert_ids`: each token names 6 different experts; among the tokens of one device (aligned blocks of 128 tokens) no expert is named more than 32 times, and in some blocks one is named exactly 32 times. partner[partner[j]] = j and partner[j] != j for every j.
All inputs are finite; a program needn't handle non-finite values.
Results may differ from the reference program's by a relative error of at most 0.017.
Values may be sent and summed in bfloat16 or wider, within the bound.
A program may use at most 192 MiB of HBM per device.

```python
import math
import jax
import jax.numpy as jnp
import numpy as np
from jax import lax

D = 2048
H = 768
TOPK = 6
EXP_DEV = 2
TOK_DEV = 128
OWNERS = 16
DP_GROUPS = 8
EXPERTS = 32
TOKENS = 16384
CAP = 32


def draw_partner(key, part):
    order = jax.random.permutation(key, OWNERS).astype(jnp.int32)
    paired = order.reshape(OWNERS // 2, 2)[:, ::-1].reshape(OWNERS)
    return jnp.zeros((OWNERS,), jnp.int32).at[order].set(paired)


def strengthened(values, own_key, source, target, shards_of, factor):
    def block_of(axis_at):
        return (jnp.arange(values.shape[axis_at]) // (values.shape[axis_at] // shards_of)).reshape((-1,) + (1,) * (values.ndim - 1 - axis_at))

    first = jax.random.permutation(own_key, shards_of)[block_of(target)]
    other_side = (block_of(target) + shards_of // 2) % shards_of
    return jnp.where((block_of(source) == first) | (block_of(source) == other_side), factor * values, values)


def levels(stream_key, shape, shards, least, top_value):
    level, own = 1.0, jax.random.fold_in(stream_key, 6)
    for dim, shards_of in shards:
        steps = jnp.exp(jax.random.uniform(jax.random.fold_in(own, dim), (shards_of,), jnp.float32, least / len(shards), top_value / len(shards)))
        level = level * jnp.repeat(steps, shape[dim] // shards_of).reshape([-1 if axis == dim else 1 for axis in range(len(shape))])
    return level


def shared_out(rng, own, number, rows, number_of, top, bound, lean):
    sequence = jax.random.permutation(rng, number_of)
    crowded, usual = load_shares(number_of, rows * top, bound, lean, True), load_shares(number_of, rows * top, bound, lean, False)
    places = jnp.arange(number_of)

    def named(sizes, rotation):
        used = int((sizes > 0).sum())
        fixed = max(1, used // 4)
        moved = fixed + (places - fixed + rotation * (used - fixed)) % max(1, number_of - fixed)
        return jnp.zeros((number_of,), jnp.int32).at[sequence[jnp.where(places < fixed, places, moved)]].set(jnp.asarray(sizes, jnp.int32))

    sizes = jnp.where(number % 4 == 0, named(crowded, number // 4), named(usual, number - number // 4 - 1))
    mixed = jax.random.permutation(jax.random.fold_in(own, 3), number_of)
    giver, sink = mixed[0:number_of // 2 * 2:2], mixed[1:number_of // 2 * 2:2]
    slack = jnp.minimum(sizes[giver] - 1, bound - sizes[sink]) // 2
    slack = jnp.where((giver == sequence[0]) | (sink == sequence[0]) | (sizes[sink] == 0), 0, jnp.maximum(slack, 0))
    moved = jax.random.randint(jax.random.fold_in(own, 4), (number_of // 2,), 0, 1 << 20) % (slack + 1)
    sizes = sizes.at[giver].add(-moved).at[sink].add(moved)
    items = jnp.searchsorted(jnp.cumsum(sizes), jnp.arange(rows * top), side="right").astype(jnp.int32)
    listing = items.reshape(top, rows).T
    listing = listing[jax.random.permutation(jax.random.fold_in(own, 1), rows)]
    rotation = jax.random.randint(jax.random.fold_in(own, 2), (rows, 1), 0, top)
    return jnp.take_along_axis(listing, (jnp.arange(top)[None, :] + rotation) % top, axis=1)


def load_shares(count, total, reach, slope, full):
    loads = [(1 << 20) // math.isqrt(rank ** slope) + 1 for rank in range(1, count + 1)]
    largest = reach if full else min(reach, max(-(-total // count), total * loads[0] // sum(loads)))
    least = 1 if total - largest >= count - 1 else 0
    counts, spare = [largest] + [least] * (count - 1), total - largest - least * (count - 1)
    while spare > 0:
        movable = [i for i in range(1, count) if counts[i] < largest] or [i for i in range(1, count) if counts[i] < reach]
        mass, left = sum([loads[i] for i in movable]), spare
        for i in movable:
            addition = min(reach - counts[i], max(1, left * loads[i] // mass), spare)
            counts[i] = counts[i] + addition
            spare = spare - addition
    return np.array(counts)


def gaussian(rng, extent, width, bound, cuts=(), held_as=jnp.bfloat16):
    loudness = levels(rng, extent, cuts, -0.22, 0.18) if cuts else 1.0
    entries = jax.random.normal(rng, extent, jnp.float32) * width * loudness
    return jnp.minimum(jnp.maximum(entries, -bound), bound).astype(held_as)


def gaussian_with(key, shape, spread, most, split, heavy, kind=jnp.bfloat16):
    values = spread * jax.random.normal(key, shape, jnp.float32)
    if split:
        values = values * levels(key, shape, split, -0.22, 0.18)
    return jnp.clip(strengthened(values, jax.random.fold_in(key, 3), *heavy), -most, most).astype(kind)


def setup_inputs(seed: int = 0) -> dict:
    key_of = jax.random.split(jax.random.key(seed), 8)
    tokens = gaussian_with(key_of[0], (TOKENS, D), 1.0, 24.0, ((0, 128),), (0, 1, 128, 5.5))
    expert_ids_keys = jax.random.split(jax.random.fold_in(key_of[1], 1), TOKENS // TOK_DEV)
    expert_ids_turns = jax.random.permutation(jax.random.fold_in(key_of[1], 3), TOKENS // TOK_DEV)
    expert_ids = jax.vmap(lambda own, number: shared_out(jax.random.fold_in(key_of[1], 2), own, number, TOK_DEV, EXPERTS, TOPK, CAP, 2))(expert_ids_keys, expert_ids_turns).reshape((TOKENS, TOPK))
    combine_weight = jnp.clip(jnp.exp(math.log(1.0) - 2.9957323 * jax.random.uniform(key_of[2], (TOKENS, TOPK), jnp.float32) ** levels(key_of[2], (TOKENS, TOPK), ((0, 128),), -0.2, 0.2)), 0.05, 1.0)
    partner = draw_partner(jax.random.fold_in(key_of[7], 71), 0)
    w_up = gaussian(key_of[4], (D, EXPERTS, H), D ** -0.5, 0.125, ((1, 16),))
    w_down = gaussian(key_of[5], (D, EXPERTS, H), H ** -0.5, 0.21875, ((1, 16),))
    out_grad = gaussian(key_of[6], (TOKENS, D), 1.0, 6.0, ((0, 128),))
    return dict(tokens=tokens, expert_ids=expert_ids, combine_weight=combine_weight, partner=partner, w_up=w_up, w_down=w_down, out_grad=out_grad)


def silu_slope(hidden_pre):
    sigma = jax.nn.sigmoid(hidden_pre)
    return sigma * (1.0 + hidden_pre * (1.0 - sigma))


def reference(tokens, expert_ids, combine_weight, partner, w_up, w_down, out_grad):
    blocks = DP_GROUPS * OWNERS
    per_block = TOK_DEV * TOPK
    named = expert_ids.reshape(blocks, per_block).astype(jnp.int32)
    onehot = (named[:, :, None] == jnp.arange(EXPERTS, dtype=jnp.int32)[None, None, :]).astype(jnp.int32)
    earlier = jnp.cumsum(onehot, axis=1) - onehot
    position = jnp.sum(earlier * onehot, axis=2).astype(jnp.int32)
    block_index = jnp.arange(blocks, dtype=jnp.int32)[:, None]
    group_index = jnp.broadcast_to(block_index // OWNERS, named.shape).astype(jnp.int32)
    within = jnp.arange(per_block, dtype=jnp.int32)[None, :]
    token_index = (block_index * TOK_DEV + within // TOPK).astype(jnp.int32)
    slot_row = ((block_index % OWNERS) * CAP + position).astype(jnp.int32)
    token_table = jnp.full((EXPERTS, DP_GROUPS, OWNERS * CAP), TOKENS, jnp.int32)
    token_table = token_table.at[named, group_index, slot_row].set(token_index)
    coef_table = jnp.zeros((EXPERTS, DP_GROUPS, OWNERS * CAP), jnp.float32)
    coef_table = coef_table.at[named, group_index, slot_row].set(
        combine_weight.reshape(blocks, per_block).astype(jnp.float32))
    padded_tokens = jnp.concatenate([tokens, jnp.zeros((1, D), tokens.dtype)], axis=0)
    padded_grad = jnp.concatenate([out_grad, jnp.zeros((1, D), out_grad.dtype)], axis=0)
    up_stack = jnp.moveaxis(w_up, 1, 0)
    down_stack = jnp.moveaxis(w_down, 1, 0)
    grad_scale = 1.0 / TOK_DEV
    slot_rows = OWNERS * CAP

    def one_expert(totals, pieces):
        out_total, grad_total = totals
        token_rows, weight, up_mat, down_mat = pieces
        flat_rows = token_rows.reshape(-1)
        weight_col = weight.reshape(-1)[:, None]
        inputs = padded_tokens[flat_rows]
        hidden_pre = jnp.dot(inputs, up_mat, preferred_element_type=jnp.float32)
        activated = jax.nn.silu(hidden_pre).astype(jnp.bfloat16)
        expert_out = jnp.dot(activated, down_mat.T, preferred_element_type=jnp.float32).astype(jnp.bfloat16)
        out_total = out_total.at[flat_rows].add(weight_col * expert_out.astype(jnp.float32), mode="drop")
        grad_out = (weight_col * padded_grad[flat_rows].astype(jnp.float32)).astype(jnp.bfloat16)
        grad_act = jnp.dot(grad_out, down_mat, preferred_element_type=jnp.float32)
        grad_pre = (grad_act * silu_slope(hidden_pre)).astype(jnp.bfloat16)
        grad_in = jnp.dot(grad_pre, up_mat.T, preferred_element_type=jnp.float32).astype(jnp.bfloat16)
        grad_total = grad_total.at[flat_rows].add(grad_in.astype(jnp.float32), mode="drop")
        input_groups = inputs.reshape(DP_GROUPS, slot_rows, D).astype(jnp.float32)
        pre_groups = grad_pre.reshape(DP_GROUPS, slot_rows, H).astype(jnp.float32)
        outg_groups = grad_out.reshape(DP_GROUPS, slot_rows, D).astype(jnp.float32)
        act_groups = activated.reshape(DP_GROUPS, slot_rows, H).astype(jnp.float32)
        part_up = (jnp.einsum("nrd,nrh->ndh", input_groups, pre_groups) * grad_scale).astype(jnp.bfloat16)
        part_down = (jnp.einsum("nrd,nrh->ndh", outg_groups, act_groups) * grad_scale).astype(jnp.bfloat16)
        part_up = lax.optimization_barrier(part_up)
        part_down = lax.optimization_barrier(part_down)
        total_up = jnp.sum(part_up.astype(jnp.float32), axis=0)
        total_down = jnp.sum(part_down.astype(jnp.float32), axis=0)
        return (out_total, grad_total), (total_up, total_down)

    start = (jnp.zeros((TOKENS, D), jnp.float32), jnp.zeros((TOKENS, D), jnp.float32))
    (out_total, grad_total), (total_up, total_down) = lax.scan(
        one_expert, start, (token_table, coef_table, up_stack, down_stack))
    column = jnp.arange(EXPERTS, dtype=jnp.int32)
    holder = column // EXP_DEV
    slot_of = column % EXP_DEV
    anchor = jnp.where(slot_of == 0, partner[holder] * EXP_DEV, column).astype(jnp.int32)
    grad_up = jnp.moveaxis(total_up[anchor], 0, 1).astype(jnp.bfloat16)
    grad_down = jnp.moveaxis(total_down[anchor], 0, 1).astype(jnp.bfloat16)
    return (out_total.astype(jnp.bfloat16), grad_total.astype(jnp.bfloat16), grad_up, grad_down)
```

```python
import functools

import jax
import jax.numpy as jnp
from jax import lax
from jax.experimental import pallas as pl
from jax.experimental.pallas import tpu as pltpu
from jax.sharding import PartitionSpec as P

MESH = pl.DeviceIdType.MESH
BF = jnp.bfloat16
F32 = jnp.float32
DMA = pltpu.SemaphoreType.DMA
SIDE = 4


class Place:
    def __init__(self):
        self.dp = lax.axis_index("dp")
        self.me = lax.axis_index("expert")
        self.y = self.me // SIDE
        self.x = lax.rem(self.me, SIDE)

    def along_y(self, step):
        return (self.dp, lax.rem(self.y + step, SIDE) * SIDE + self.x)

    def along_x(self, step):
        return (self.dp, self.y * SIDE + lax.rem(self.x + step, SIDE))

    def first(self, half, step):
        return self.along_y(step) if half == 0 else self.along_x(step)

    def second(self, half, step):
        return self.along_x(step) if half == 0 else self.along_y(step)

    def first_at(self, half):
        return self.y if half == 0 else self.x

    def second_at(self, half):
        return self.x if half == 0 else self.y

    def greet(self):
        barrier = pltpu.get_barrier_semaphore()
        for step in (1, 2, 3):
            for peer in (self.along_y(step), self.along_x(step)):
                pl.semaphore_signal(barrier, inc=1, device_id=peer, device_id_type=MESH)
        pl.semaphore_wait(barrier, 6)


def send(src, dst, send_sem, recv_sem, peer):
    copy = pltpu.make_async_remote_copy(
        src_ref=src, dst_ref=dst, send_sem=send_sem, recv_sem=recv_sem, device_id=peer, device_id_type=MESH
    )
    copy.start()
    return copy


def dot(a, b, over_a=1, over_b=0):
    return lax.dot_general(a, b, (((over_a,), (over_b,)), ((), ())), preferred_element_type=F32)


def forth_kernel(
    cap, chosen, scale,
    route, tok, og, wu_hbm, wd_hbm,
    o_hbm, gi_hbm, dw_hbm, pick,
    rt, rank, wt, p1, st, xg, wu, wd, wbuf, wcol, slope, actw, gp, ov, gv, dwv,
    rt_s, rt_r, p1_s, p1_r, p2_s, p2_r, w_sem, o_sem, g_sem, dw_sem,
):
    at = Place()
    x, y, me = at.x, at.y, at.me
    toks = tok.shape[0]
    half_w = tok.shape[1] // 2
    hidden = wu.shape[2]
    rows = SIDE * SIDE * cap
    chunk = wbuf.shape[1]
    steps = (1, 2, 3)

    at.greet()
    rt[x * SIDE + y] = route[...]
    sends = []
    first = [
        send(route, rt.at[x * SIDE + y], rt_s.at[0, k], rt_r.at[0, k], at.along_y(k)) for k in steps
    ]

    def phase1(t):
        src = (tok, og)[t]
        out = []
        for h in (0, 1):
            for k in steps:
                out.append(
                    send(
                        src.at[:, pl.ds(h * half_w, half_w)],
                        p1.at[t, h, at.first_at(h)],
                        p1_s.at[t, h, k], p1_r.at[t, h, k], at.first(h, k),
                    )
                )
        return out

    def own1(t):
        src = (tok, og)[t]
        for h in (0, 1):
            p1[t, h, at.first_at(h)] = src[:, h * half_w : (h + 1) * half_w]

    arriving = [phase1(0), None]
    own1(0)
    for c in first:
        c.wait()
    block = rt.at[pl.ds(x * SIDE, SIDE)]
    second = [send(block, block, rt_s.at[1, k], rt_r.at[1, k], at.along_x(k)) for k in steps]

    def weights(hbm, vmem, lo, hi):
        def fetch(i):
            slot = lax.rem(i, 2)
            return pltpu.make_async_copy(
                hbm.at[pl.ds(pl.multiple_of(i * chunk, chunk), chunk)], wbuf.at[slot], w_sem.at[slot]
            )

        fetch(lo).start()

        def turn(i, carry):
            @pl.when(i + 1 < hi)
            def _():
                fetch(i + 1).start()

            fetch(i).wait()
            vmem[:, pl.ds(pl.multiple_of(i * chunk, chunk), chunk), :] = jnp.swapaxes(
                wbuf[lax.rem(i, 2)], 0, 1
            )
            return carry

        lax.fori_loop(lo, hi, turn, 0)

    n_chunks = wu.shape[1] // chunk
    for c in second:
        c.wait()

    before = (
        lax.broadcasted_iota(jnp.int32, (toks, toks), 0) < lax.broadcasted_iota(jnp.int32, (toks, toks), 1)
    ).astype(F32).astype(BF)
    n_exp = rank.shape[1]
    owners = n_exp // 2
    line = lax.broadcasted_iota(jnp.int32, (n_exp, toks), 0)
    expert = (lax.rem(line, owners) * 2 + line // owners).astype(F32)

    def ranks(n, carry):
        r = rt[n]
        named = jnp.zeros((n_exp, toks), F32)
        weight = jnp.zeros((n_exp, toks), F32)
        for k in range(chosen):
            m = (r[k : k + 1, :] == expert).astype(F32)
            named += m
            weight += m * r[8 + k : 9 + k, :]
        pos = dot(named.astype(BF), before)
        rank[n] = jnp.where(named > 0, pos, -1.0)
        wt[n] = weight
        return carry

    lax.fori_loop(0, SIDE * SIDE, ranks, 0)
    place = lax.broadcasted_iota(jnp.int32, (cap, toks), 0).astype(F32)

    def picks(j, carry):
        for h in (0, 1):
            n = x * SIDE + j if h == 0 else j * SIDE + y
            for s in (0, 1):
                for d in range(SIDE):
                    owner = y * SIDE + d if h == 0 else d * SIDE + x
                    q = rank[n, pl.ds(s * owners + owner, 1), :]
                    pick[h, j, (s * SIDE + d) * cap : (s * SIDE + d + 1) * cap, :] = (
                        (place == q).astype(F32).astype(BF)
                    )
        return carry

    lax.fori_loop(0, SIDE, picks, 0)

    def slot_weights(n, carry):
        for s in (0, 1):
            q = rank[n, pl.ds(s * owners + me, 1), :]
            w = wt[n, pl.ds(s * owners + me, 1), :]
            col = jnp.sum(jnp.where(place == q, w, 0.0), axis=1, keepdims=True)
            row = (lax.rem(n, SIDE) * SIDE + n // SIDE) * cap
            wcol[s, pl.ds(pl.multiple_of(row, cap), cap), :] = jnp.broadcast_to(col, (cap, toks))
        return carry

    lax.fori_loop(0, SIDE * SIDE, slot_weights, 0)

    weights(wu_hbm, wu, 0, n_chunks // 2)
    arriving[1] = phase1(1)
    own1(1)
    weights(wu_hbm, wu, n_chunks // 2, n_chunks)

    def stage(t):
        for h in (0, 1):
            mine = at.second_at(h)

            def turn(j, carry):
                got = dot(pick[h, j], p1[t, h, j]).astype(BF).reshape(2, SIDE, cap, half_w)
                st[t, h, :, :, j] = got
                return carry

            lax.fori_loop(0, SIDE, turn, 0)
            for s in (0, 1):
                own = st[t, h, s, pl.ds(mine, 1)].reshape(SIDE, cap, half_w)
                if h == 0:
                    xg[t, s, h, :, pl.ds(x, 1)] = own.reshape(SIDE, 1, cap, half_w)
                else:
                    xg[t, s, h, pl.ds(y, 1)] = own.reshape(1, SIDE, cap, half_w)

    def phase2(t, s):
        out = []
        for h in (0, 1):
            for k in steps:
                peer_at = lax.rem(at.second_at(h) + k, SIDE)
                dst = xg.at[t, s, h, :, x] if h == 0 else xg.at[t, s, h, y]
                out.append(
                    send(st.at[t, h, s, peer_at], dst, p2_s.at[t, s, h, k], p2_r.at[t, s, h, k], at.second(h, k))
                )
        return out

    moving = {}
    for c in arriving[0]:
        c.wait_recv()
    stage(0)
    moving[0, 0] = phase2(0, 0)
    for c in arriving[1]:
        c.wait_recv()
    stage(1)
    moving[1, 0] = phase2(1, 0)
    moving[0, 1] = phase2(0, 1)
    moving[1, 1] = phase2(1, 1)
    weights(wd_hbm, wd, 0, n_chunks)

    tile = 256
    h_tiles = hidden // tile
    d_tiles = 2 * half_w // tile
    per_half = half_w // tile

    def inputs(t, s, h):
        return xg[t, s, h].reshape(rows, half_w)

    def forward(s):
        def turn(n, carry):
            cols = pl.ds(pl.multiple_of(n * tile, tile), tile)
            pre = dot(inputs(0, s, 0), wu[s, 0:half_w, cols]) + dot(inputs(0, s, 1), wu[s, half_w : 2 * half_w, cols])
            w = wcol[s, :, 0:1]
            sig = 1.0 / (1.0 + jnp.exp(-pre))
            actw[s, :, cols] = (pre * sig * w).astype(BF)
            slope[s, :, cols] = sig * (1.0 + pre * (1.0 - sig)) * w
            return carry

        lax.fori_loop(0, h_tiles, turn, 0)

        def out(i, carry):
            got = dot(actw[s], wd[s, pl.ds(pl.multiple_of(i * tile, tile), tile), :], 1, 1)
            ov[s, i // per_half, :, pl.ds(pl.multiple_of(lax.rem(i, per_half) * tile, tile), tile)] = got.astype(BF)
            return carry

        lax.fori_loop(0, d_tiles, out, 0)
        copy = pltpu.make_async_copy(ov.at[s], o_hbm.at[s], o_sem.at[s])
        copy.start()
        return copy

    def backward(s):
        def turn(n, carry):
            cols = pl.ds(pl.multiple_of(n * tile, tile), tile)
            ga = dot(inputs(1, s, 0), wd[s, 0:half_w, cols]) + dot(inputs(1, s, 1), wd[s, half_w : 2 * half_w, cols])
            gp[s, :, cols] = (ga * slope[s, :, cols]).astype(BF)
            return carry

        lax.fori_loop(0, h_tiles, turn, 0)

        def grad(i, carry):
            got = dot(gp[s], wu[s, pl.ds(pl.multiple_of(i * tile, tile), tile), :], 1, 1)
            gv[s, i // per_half, :, pl.ds(pl.multiple_of(lax.rem(i, per_half) * tile, tile), tile)] = got.astype(BF)
            return carry

        def drain(t, i):
            slot = lax.rem(i, 2)
            return pltpu.make_async_copy(
                dwv.at[t, slot],
                dw_hbm.at[s, pl.ds(pl.multiple_of(i * tile, tile), tile), pl.ds(t * hidden, hidden)],
                dw_sem.at[t, slot],
            )

        def dw(i, carry):
            cols = pl.ds(pl.multiple_of(lax.rem(i, per_half) * tile, tile), tile)
            for t, other in ((0, gp), (1, actw)):
                left = xg[t, s, i // per_half, :, :, :, cols].reshape(rows, tile)
                got = dot(left, other[s], 0, 0) * scale

                @pl.when(i >= 2)
                def _():
                    drain(t, i - 2).wait()

                dwv[t, lax.rem(i, 2)] = got.astype(BF)
                drain(t, i).start()
            return carry

        lax.fori_loop(0, d_tiles, dw, 0)
        for i in (d_tiles - 2, d_tiles - 1):
            for t in (0, 1):
                drain(t, i).wait()
        lax.fori_loop(0, d_tiles, grad, 0)
        copy = pltpu.make_async_copy(gv.at[s], gi_hbm.at[s], g_sem.at[s])
        copy.start()
        return copy

    local = []
    for s in (0, 1):
        for c in moving[0, s]:
            c.wait_recv()
        local.append(forward(s))
        for c in moving[1, s]:
            c.wait_recv()
        local.append(backward(s))
    for c in arriving[0] + arriving[1]:
        c.wait_send()
    for t in (0, 1):
        for s in (0, 1):
            for c in moving[t, s]:
                c.wait_send()
    for c in local:
        c.wait()


def back_kernel(cap, o_hbm, gi_hbm, pick, out, ig, rec, dense, part, own_sem, r1_s, r1_r, r2_s, r2_r):
    at = Place()
    steps = (1, 2, 3)
    half_w = out.shape[1] // 2
    toks = out.shape[0]
    at.greet()

    def block(t, s, h, other):
        src = (o_hbm, gi_hbm)[t]
        return src.at[s, h, :, other] if h == 0 else src.at[s, h, other]

    def phase1(t, s):
        copies = []
        for h in (0, 1):
            mine = at.second_at(h)
            dst = rec.at[t, h, :, s, mine]
            own = pltpu.make_async_copy(block(t, s, h, mine), dst, own_sem.at[t, s, h])
            own.start()
            for k in steps:
                peer_at = lax.rem(mine + k, SIDE)
                copies.append(
                    send(block(t, s, h, peer_at), dst, r1_s.at[t, s, h, k], r1_r.at[t, s, h, k], at.second(h, k))
                )
            copies.append(own)
        return copies

    def arrived(copies):
        for c in copies:
            if c.is_remote:
                c.wait_recv()
            else:
                c.wait()

    def token_sums(t, h, j):
        return dot(pick[h, j], rec[t, h, j].reshape(2 * SIDE * cap, half_w), 0, 0)

    moving = {}
    second = {0: [], 1: []}

    def phase2(t):
        for h in (0, 1):
            mine = at.first_at(h)
            for k in steps:
                j = lax.rem(mine + k, SIDE)
                dense[t, h, k - 1] = token_sums(t, h, j).astype(BF)
                second[t].append(
                    send(dense.at[t, h, k - 1], part.at[t, h, k - 1], r2_s.at[t, h, k], r2_r.at[t, h, k], at.first(h, k))
                )

    def finish(t):
        result = (out, ig)[t]
        for h in (0, 1):
            total = token_sums(t, h, at.first_at(h))
            for c in second[t][3 * h : 3 * h + 3]:
                c.wait_recv()
            for k in steps:
                total = total + part[t, h, k - 1].astype(F32)
            result[:, h * half_w : (h + 1) * half_w] = total.astype(BF)

    moving[0, 0] = phase1(0, 0)
    moving[0, 1] = phase1(0, 1)
    arrived(moving[0, 0])
    moving[1, 0] = phase1(1, 0)
    arrived(moving[0, 1])
    moving[1, 1] = phase1(1, 1)
    phase2(0)
    arrived(moving[1, 0])
    arrived(moving[1, 1])
    phase2(1)
    finish(0)
    finish(1)
    for copies in list(moving.values()) + list(second.values()):
        for c in copies:
            if c.is_remote:
                c.wait_send()


def body(tokens, expert_ids, combine_weight, partner, w_up, w_down, out_grad):
    toks, chosen = expert_ids.shape
    width = tokens.shape[1]
    half_w = width // 2
    hidden = w_up.shape[2]
    owners = SIDE * SIDE
    cap = toks * chosen * 4 // (3 * 2 * owners)
    rows = owners * cap
    pad = jnp.zeros((8 - chosen, toks), F32)
    route = jnp.concatenate([expert_ids.T.astype(F32), pad, combine_weight.T, pad], axis=0)
    any_ = pl.BlockSpec(memory_space=pl.ANY)
    vmem = pl.BlockSpec(memory_space=pltpu.VMEM)
    o_buf, gi_buf, dw, pick = pl.pallas_call(
        functools.partial(forth_kernel, cap, chosen, 1.0 / toks),
        out_shape=(
            jax.ShapeDtypeStruct((2, 2, rows, half_w), BF),
            jax.ShapeDtypeStruct((2, 2, rows, half_w), BF),
            jax.ShapeDtypeStruct((2, width, 2 * hidden), BF),
            jax.ShapeDtypeStruct((2, SIDE, 2 * SIDE * cap, toks), BF),
        ),
        in_specs=[vmem, vmem, vmem, any_, any_],
        out_specs=(any_, any_, any_, vmem),
        scratch_shapes=[
            pltpu.VMEM((owners, 16, toks), F32),
            pltpu.VMEM((owners, 2 * owners, toks), F32),
            pltpu.VMEM((owners, 2 * owners, toks), F32),
            pltpu.VMEM((2, 2, SIDE, toks, half_w), BF),
            pltpu.VMEM((2, 2, 2, SIDE, SIDE, cap, half_w), BF),
            pltpu.VMEM((2, 2, 2, SIDE, SIDE, cap, half_w), BF),
            pltpu.VMEM((2, width, hidden), BF),
            pltpu.VMEM((2, width, hidden), BF),
            pltpu.VMEM((2, 128, 2, hidden), BF),
            pltpu.VMEM((2, rows, toks), F32),
            pltpu.VMEM((2, rows, hidden), F32),
            pltpu.VMEM((2, rows, hidden), BF),
            pltpu.VMEM((2, rows, hidden), BF),
            pltpu.VMEM((2, 2, rows, half_w), BF),
            pltpu.VMEM((2, 2, rows, half_w), BF),
            pltpu.VMEM((2, 2, 256, hidden), BF),
            DMA((2, 4)), DMA((2, 4)),
            DMA((2, 2, 4)), DMA((2, 2, 4)),
            DMA((2, 2, 2, 4)), DMA((2, 2, 2, 4)),
            DMA((2,)), DMA((2,)), DMA((2,)), DMA((2, 2)),
        ],
        compiler_params=pltpu.CompilerParams(
            collective_id=0, has_side_effects=True, vmem_limit_bytes=60 << 20
        ),
    )(route, tokens, out_grad, w_up, w_down)

    summed = [lax.psum_scatter(dw[s], "dp", scatter_dimension=0, tiled=True) for s in (0, 1)]

    shape = (2, 2, SIDE, SIDE, cap, half_w)
    output, input_grad = pl.pallas_call(
        functools.partial(back_kernel, cap),
        out_shape=(
            jax.ShapeDtypeStruct((toks, width), BF),
            jax.ShapeDtypeStruct((toks, width), BF),
        ),
        in_specs=[any_, any_, vmem],
        out_specs=(vmem, vmem),
        scratch_shapes=[
            pltpu.VMEM((2, 2, SIDE, 2, SIDE, cap, half_w), BF),
            pltpu.VMEM((2, 2, SIDE - 1, toks, half_w), BF),
            pltpu.VMEM((2, 2, SIDE - 1, toks, half_w), BF),
            DMA((2, 2, 2)),
            DMA((2, 2, 2, 4)), DMA((2, 2, 2, 4)),
            DMA((2, 2, 4)), DMA((2, 2, 4)),
        ],
        compiler_params=pltpu.CompilerParams(
            collective_id=1, has_side_effects=True, vmem_limit_bytes=40 << 20
        ),
    )(o_buf.reshape(shape), gi_buf.reshape(shape), pick)

    n_rows = summed[0].shape[0]
    spread = lax.all_to_all(
        summed[0].reshape(owners, n_rows // owners, 2 * hidden), "expert", split_axis=0, concat_axis=0, tiled=True
    )
    choose = (partner[:, None] == jnp.arange(owners, dtype=jnp.int32)[None, :]).astype(BF)
    ordered = lax.dot_general(
        choose, spread, (((1,), (0,)), ((), ())), preferred_element_type=F32
    ).astype(BF)
    moved = lax.all_to_all(ordered, "expert", split_axis=0, concat_axis=0, tiled=True).reshape(n_rows, 2 * hidden)
    grad_up = jnp.stack([moved[:, :hidden], summed[1][:, :hidden]], axis=1)
    grad_down = jnp.stack([moved[:, hidden:], summed[1][:, hidden:]], axis=1)
    return (output, input_grad, grad_up, grad_down)


def solution(mesh):
    return jax.shard_map(
        body,
        mesh=mesh,
        in_specs=(
            P(("dp", "expert"), None),
            P(("dp", "expert"), None),
            P(("dp", "expert"), None),
            P(),
            P(None, "expert", None),
            P(None, "expert", None),
            P(("dp", "expert"), None),
        ),
        out_specs=(
            P(("dp", "expert"), None),
            P(("dp", "expert"), None),
            P("dp", "expert", None),
            P("dp", "expert", None),
        ),
        check_vma=False,
    )
```

```python
import functools

import jax
import jax.numpy as jnp
from jax import lax
from jax.experimental import pallas as pl
from jax.experimental.pallas import tpu as pltpu
from jax.sharding import PartitionSpec as P

MESH = pl.DeviceIdType.MESH
BF = jnp.bfloat16
F32 = jnp.float32
DMA = pltpu.SemaphoreType.DMA
SIDE = 4


class Place:
    def __init__(self):
        self.dp = lax.axis_index("dp")
        self.me = lax.axis_index("expert")
        self.y = self.me // SIDE
        self.x = lax.rem(self.me, SIDE)
        self.z = self.dp // 2
        self.core = lax.rem(self.dp, 2)

    def along_y(self, step):
        return (self.dp, lax.rem(self.y + step, SIDE) * SIDE + self.x)

    def along_x(self, step):
        return (self.dp, self.y * SIDE + lax.rem(self.x + step, SIDE))

    def first(self, half, step):
        return self.along_y(step) if half == 0 else self.along_x(step)

    def second(self, half, step):
        return self.along_x(step) if half == 0 else self.along_y(step)

    def first_at(self, half):
        return self.y if half == 0 else self.x

    def second_at(self, half):
        return self.x if half == 0 else self.y

    def along_z(self, step):
        return (lax.rem(self.z + step, SIDE) * 2 + self.core, self.me)

    def other_core(self):
        return (self.z * 2 + 1 - self.core, self.me)

    def greet(self):
        barrier = pltpu.get_barrier_semaphore()
        peers = [self.other_core()]
        for step in (1, 2, 3):
            peers += [self.along_y(step), self.along_x(step), self.along_z(step)]
        for peer in peers:
            pl.semaphore_signal(barrier, inc=1, device_id=peer, device_id_type=MESH)
        pl.semaphore_wait(barrier, len(peers))


def send(src, dst, send_sem, recv_sem, peer):
    copy = pltpu.make_async_remote_copy(
        src_ref=src, dst_ref=dst, send_sem=send_sem, recv_sem=recv_sem, device_id=peer, device_id_type=MESH
    )
    copy.start()
    return copy


def dot(a, b, over_a=1, over_b=0):
    return lax.dot_general(a, b, (((over_a,), (over_b,)), ((), ())), preferred_element_type=F32)


def kernel(
    cap, chosen, scale,
    route, tok, og, wu_hbm, wd_hbm,
    out, ig, g0_hbm, g1_hbm, rec, cr, zr,
    rt, rank, wt, pick, p1, st, xg, wu, wd, wbuf, wcol, slope, right, part, rbuf, own, xs, ld,
    rt_s, rt_r, p1_s, p1_r, p2_s, p2_r, w_sem, r1_s, r1_r, own_sem, r2_s, r2_r, rb_sem,
    c_s, c_r, z_s, z_r, ld_sem, g_sem,
):
    at = Place()
    x, y, me = at.x, at.y, at.me
    toks = tok.shape[0]
    half_w = tok.shape[1] // 2
    hidden = wu.shape[2]
    rows = SIDE * SIDE * cap
    chunk = wbuf.shape[1]
    steps = (1, 2, 3)

    at.greet()
    rt[x * SIDE + y] = route[...]
    sends = []
    first = [
        send(route, rt.at[x * SIDE + y], rt_s.at[0, k], rt_r.at[0, k], at.along_y(k)) for k in steps
    ]

    def phase1(t):
        src = (tok, og)[t]
        out = []
        for h in (0, 1):
            for k in steps:
                out.append(
                    send(
                        src.at[:, pl.ds(h * half_w, half_w)],
                        p1.at[t, h, at.first_at(h)],
                        p1_s.at[t, h, k], p1_r.at[t, h, k], at.first(h, k),
                    )
                )
        return out

    def own1(t):
        src = (tok, og)[t]
        for h in (0, 1):
            p1[t, h, at.first_at(h)] = src[:, h * half_w : (h + 1) * half_w]

    arriving = [phase1(0), None]
    own1(0)
    for c in first:
        c.wait()
    block = rt.at[pl.ds(x * SIDE, SIDE)]
    second = [send(block, block, rt_s.at[1, k], rt_r.at[1, k], at.along_x(k)) for k in steps]

    def weights(hbm, vmem, lo, hi):
        def fetch(i):
            slot = lax.rem(i, 2)
            return pltpu.make_async_copy(
                hbm.at[pl.ds(pl.multiple_of(i * chunk, chunk), chunk)], wbuf.at[slot], w_sem.at[slot]
            )

        fetch(lo).start()

        def turn(i, carry):
            @pl.when(i + 1 < hi)
            def _():
                fetch(i + 1).start()

            fetch(i).wait()
            vmem[:, pl.ds(pl.multiple_of(i * chunk, chunk), chunk), :] = jnp.swapaxes(
                wbuf[lax.rem(i, 2)], 0, 1
            )
            return carry

        lax.fori_loop(lo, hi, turn, 0)

    n_chunks = wu.shape[1] // chunk
    for c in second:
        c.wait()

    before = (
        lax.broadcasted_iota(jnp.int32, (toks, toks), 0) < lax.broadcasted_iota(jnp.int32, (toks, toks), 1)
    ).astype(F32).astype(BF)
    n_exp = rank.shape[1]
    owners = n_exp // 2
    line = lax.broadcasted_iota(jnp.int32, (n_exp, toks), 0)
    expert = (lax.rem(line, owners) * 2 + line // owners).astype(F32)

    def ranks(n, carry):
        r = rt[n]
        named = jnp.zeros((n_exp, toks), F32)
        weight = jnp.zeros((n_exp, toks), F32)
        for k in range(chosen):
            m = (r[k : k + 1, :] == expert).astype(F32)
            named += m
            weight += m * r[8 + k : 9 + k, :]
        pos = dot(named.astype(BF), before)
        rank[n] = jnp.where(named > 0, pos, -1.0)
        wt[n] = weight
        return carry

    lax.fori_loop(0, SIDE * SIDE, ranks, 0)
    place = lax.broadcasted_iota(jnp.int32, (cap, toks), 0).astype(F32)

    def picks(j, carry):
        for h in (0, 1):
            n = x * SIDE + j if h == 0 else j * SIDE + y
            for s in (0, 1):
                for d in range(SIDE):
                    owner = y * SIDE + d if h == 0 else d * SIDE + x
                    q = rank[n, pl.ds(s * owners + owner, 1), :]
                    pick[h, j, (s * SIDE + d) * cap : (s * SIDE + d + 1) * cap, :] = (
                        (place == q).astype(F32).astype(BF)
                    )
        return carry

    lax.fori_loop(0, SIDE, picks, 0)

    def slot_weights(n, carry):
        for s in (0, 1):
            q = rank[n, pl.ds(s * owners + me, 1), :]
            w = wt[n, pl.ds(s * owners + me, 1), :]
            col = jnp.sum(jnp.where(place == q, w, 0.0), axis=1, keepdims=True)
            row = (lax.rem(n, SIDE) * SIDE + n // SIDE) * cap
            wcol[s, pl.ds(pl.multiple_of(row, cap), cap), :] = jnp.broadcast_to(col, (cap, toks))
        return carry

    lax.fori_loop(0, SIDE * SIDE, slot_weights, 0)

    weights(wu_hbm, wu, 0, n_chunks // 4)
    arriving[1] = phase1(1)
    own1(1)
    weights(wu_hbm, wu, n_chunks // 4, n_chunks)

    def stage(t):
        for h in (0, 1):
            mine = at.second_at(h)

            def turn(j, carry):
                got = dot(pick[h, j], p1[t, h, j]).astype(BF).reshape(2, SIDE, cap, half_w)
                st[t, h, :, :, j] = got
                return carry

            lax.fori_loop(0, SIDE, turn, 0)
            for s in (0, 1):
                own = st[t, h, s, pl.ds(mine, 1)].reshape(SIDE, cap, half_w)
                if h == 0:
                    xg[t, s, h, :, pl.ds(x, 1)] = own.reshape(SIDE, 1, cap, half_w)
                else:
                    xg[t, s, h, pl.ds(y, 1)] = own.reshape(1, SIDE, cap, half_w)

    def phase2(t, s):
        out = []
        for h in (0, 1):
            for k in steps:
                peer_at = lax.rem(at.second_at(h) + k, SIDE)
                dst = xg.at[t, s, h, :, x] if h == 0 else xg.at[t, s, h, y]
                out.append(
                    send(st.at[t, h, s, peer_at], dst, p2_s.at[t, s, h, k], p2_r.at[t, s, h, k], at.second(h, k))
                )
        return out

    moving = {}
    for c in arriving[0]:
        c.wait_recv()
    stage(0)
    moving[0, 0] = phase2(0, 0)
    weights(wd_hbm, wd, 0, n_chunks // 2)
    for c in arriving[1]:
        c.wait_recv()
    stage(1)
    moving[1, 0] = phase2(1, 0)
    moving[0, 1] = phase2(0, 1)
    moving[1, 1] = phase2(1, 1)
    weights(wd_hbm, wd, n_chunks // 2, n_chunks)

    tile = 256
    h_tiles = hidden // tile
    d_tiles = 2 * half_w // tile
    per_half = half_w // tile

    def inputs(t, s, h):
        return xg[t, s, h].reshape(rows, half_w)

    def put(i, got, dst):
        cols = pl.ds(pl.multiple_of(lax.rem(i, per_half) * tile, tile), tile)
        dst[i // per_half, :, :, :, cols] = got.astype(BF).reshape(SIDE, SIDE, cap, tile)

    def forward(s):
        def turn(n, carry):
            cols = pl.ds(pl.multiple_of(n * tile, tile), tile)
            pre = dot(inputs(0, s, 0), wu[s, 0:half_w, cols]) + dot(inputs(0, s, 1), wu[s, half_w : 2 * half_w, cols])
            w = wcol[s, :, 0:1]
            sig = 1.0 / (1.0 + jnp.exp(-pre))
            right[1, s, :, cols] = (pre * sig * w).astype(BF)
            slope[s, :, cols] = sig * (1.0 + pre * (1.0 - sig)) * w
            return carry

        lax.fori_loop(0, h_tiles, turn, 0)
        for c in moving[0, s]:
            c.wait_send()

        def result(i, carry):
            put(i, dot(right[1, s], wd[s, pl.ds(pl.multiple_of(i * tile, tile), tile), :], 1, 1), st.at[0, :, s])
            return carry

        lax.fori_loop(0, d_tiles, result, 0)

    def core_copy(s, n, zz):
        return pltpu.make_async_remote_copy(
            src_ref=xs.at[n % 2], dst_ref=cr.at[s, zz], send_sem=c_s.at[s, n], recv_sem=c_r.at[s, n],
            device_id=at.other_core(), device_id_type=MESH,
        )

    def gradient_tile(s, i, dst):
        cols = pl.ds(pl.multiple_of(lax.rem(i, per_half) * tile, tile), tile)

        def turn(t, carry):
            left = xg[t, s, i // per_half, :, :, :, cols].reshape(rows, tile)
            got = dot(left, right[t, s], 0, 0) * scale
            dst[:, pl.ds(pl.multiple_of(t * hidden, 128), hidden)] = got.astype(BF)
            return carry

        lax.fori_loop(0, 2, turn, 0)

    quarters = (2, 1, 3, 0)
    z_moving = {0: [], 1: []}

    def pair_sum(s, n):
        step = quarters[n]
        zz = lax.rem(at.z + step, SIDE)
        own[s, zz] = (own[s, zz].astype(F32) + ld[n % 2].astype(F32)).astype(BF)
        if step:
            z_moving[s].append(
                send(own.at[s, zz], zr.at[s, step - 1], z_s.at[s, step], z_r.at[s, step], at.along_z(step))
            )

    def fetch_pair(s, n):
        zz = lax.rem(at.z + quarters[n], SIDE)
        core_copy(s, n, zz).wait_recv()
        copy = pltpu.make_async_copy(cr.at[s, zz], ld.at[n % 2], ld_sem.at[n % 2])
        copy.start()
        return copy

    def backward(s):
        def turn(n, carry):
            cols = pl.ds(pl.multiple_of(n * tile, tile), tile)
            ga = dot(inputs(1, s, 0), wd[s, 0:half_w, cols]) + dot(inputs(1, s, 1), wd[s, half_w : 2 * half_w, cols])
            right[0, s, :, cols] = (ga * slope[s, :, cols]).astype(BF)
            return carry

        lax.fori_loop(0, h_tiles, turn, 0)
        for n, step in enumerate(quarters):
            zz = lax.rem(at.z + step, SIDE)
            if n >= 2:
                core_copy(s, n - 2, zz).wait_send()
            gradient_tile(s, zz * 2 + 1 - at.core, xs.at[n % 2])
            core_copy(s, n, zz).start()
            if n:
                got = fetch_pair(s, n - 1)
            gradient_tile(s, zz * 2 + at.core, own.at[s, zz])
            if n:
                got.wait()
                pair_sum(s, n - 1)

        def grad(i, carry):
            put(i, dot(right[0, s], wu[s, pl.ds(pl.multiple_of(i * tile, tile), tile), :], 1, 1), xg.at[1, s])
            return carry

        lax.fori_loop(0, d_tiles, grad, 0)
        fetch_pair(s, 3).wait()
        pair_sum(s, 3)
        for n in (2, 3):
            core_copy(s, n, 0).wait_send()

    def result_rows(t, s, h, other):
        block = st.at[0, h, s] if t == 0 else xg.at[1, s, h]
        return block.at[:, other] if h == 0 else block.at[other]

    def return1(t, s):
        copies = []
        for h in (0, 1):
            mine = at.second_at(h)
            dst = rec.at[t, h, :, s, mine]
            kept = pltpu.make_async_copy(result_rows(t, s, h, mine), dst, own_sem.at[t, s, h])
            kept.start()
            for k in steps:
                peer_at = lax.rem(mine + k, SIDE)
                copies.append(
                    send(result_rows(t, s, h, peer_at), dst, r1_s.at[t, s, h, k], r1_r.at[t, s, h, k], at.second(h, k))
                )
            copies.append(kept)
        return copies

    returning = {}
    for s in (0, 1):
        for c in moving[0, s]:
            c.wait_recv()
        forward(s)
        if s == 1:
            returning[0, 1] = return1(0, 1)
        for c in moving[1, s]:
            c.wait_recv()
        if s == 0:
            returning[0, 0] = return1(0, 0)
        backward(s)
        returning[1, s] = return1(1, s)

    def arrived(copies):
        for c in copies:
            if c.is_remote:
                c.wait_recv()
            else:
                c.wait()

    last = {0: [], 1: []}

    def return2(t):
        items = [(h, k) for h in (0, 1) for k in (1, 2, 3, 0)]

        def fetch(n):
            h, k = items[n]
            copy = pltpu.make_async_copy(
                rec.at[t, h, lax.rem(at.first_at(h) + k, SIDE)], rbuf.at[n % 2], rb_sem.at[n % 2]
            )
            copy.start()
            return copy

        ahead = fetch(0)
        for n, (h, k) in enumerate(items):
            ahead.wait()
            if n + 1 < len(items):
                ahead = fetch(n + 1)
            j = lax.rem(at.first_at(h) + k, SIDE)
            got = dot(pick[h, j], rbuf[n % 2].reshape(2 * SIDE * cap, half_w), 0, 0)
            p1[t, h, k] = got.astype(BF)
            if k:
                last[t].append(
                    send(p1.at[t, h, k], part.at[t, h, k - 1], r2_s.at[t, h, k], r2_r.at[t, h, k], at.first(h, k))
                )

    def finish(t):
        result = (out, ig)[t]
        for c in last[t]:
            c.wait_recv()
        for h in (0, 1):
            total = p1[t, h, 0].astype(F32)
            for k in steps:
                total = total + part[t, h, k - 1].astype(F32)
            result[:, h * half_w : (h + 1) * half_w] = total.astype(BF)

    def gradients(s):
        total = own[s, at.z].astype(F32)
        for k in steps:
            z_moving[s][(2, 1, 3).index(k)].wait_recv()
            copy = pltpu.make_async_copy(zr.at[s, k - 1], ld.at[k % 2], ld_sem.at[k % 2])
            copy.start()
            copy.wait()
            total = total + ld[k % 2].astype(F32)
        xs[s] = total.astype(BF)
        copy = pltpu.make_async_copy(xs.at[s], (g0_hbm, g1_hbm)[s], g_sem.at[s])
        copy.start()
        return copy

    arrived(returning[0, 0])
    arrived(returning[0, 1])
    return2(0)
    written = [gradients(0)]
    arrived(returning[1, 0])
    arrived(returning[1, 1])
    return2(1)
    finish(0)
    finish(1)
    written.append(gradients(1))
    for c in written:
        c.wait()
    for c in arriving[0] + arriving[1] + moving[1, 0] + moving[1, 1]:
        c.wait_send()
    for copies in list(returning.values()) + list(last.values()) + list(z_moving.values()):
        for c in copies:
            if c.is_remote:
                c.wait_send()


def body(tokens, expert_ids, combine_weight, partner, w_up, w_down, out_grad):
    toks, chosen = expert_ids.shape
    width = tokens.shape[1]
    half_w = width // 2
    hidden = w_up.shape[2]
    owners = SIDE * SIDE
    cap = toks * chosen * 4 // (3 * 2 * owners)
    rows = owners * cap
    pad = jnp.zeros((8 - chosen, toks), F32)
    route = jnp.concatenate([expert_ids.T.astype(F32), pad, combine_weight.T, pad], axis=0)
    any_ = pl.BlockSpec(memory_space=pl.ANY)
    vmem = pl.BlockSpec(memory_space=pltpu.VMEM)
    n_rows = width // (2 * SIDE)
    output, input_grad, first_grad, second_grad, *_ = pl.pallas_call(
        functools.partial(kernel, cap, chosen, 1.0 / toks),
        out_shape=(
            jax.ShapeDtypeStruct((toks, width), BF),
            jax.ShapeDtypeStruct((toks, width), BF),
            jax.ShapeDtypeStruct((n_rows, 2 * hidden), BF),
            jax.ShapeDtypeStruct((n_rows, 2 * hidden), BF),
            jax.ShapeDtypeStruct((2, 2, SIDE, 2, SIDE, cap, half_w), BF),
            jax.ShapeDtypeStruct((2, SIDE, n_rows, 2 * hidden), BF),
            jax.ShapeDtypeStruct((2, SIDE - 1, n_rows, 2 * hidden), BF),
        ),
        in_specs=[vmem, vmem, vmem, any_, any_],
        out_specs=(vmem, vmem, any_, any_, any_, any_, any_),
        scratch_shapes=[
            pltpu.VMEM((owners, 16, toks), F32),
            pltpu.VMEM((owners, 2 * owners, toks), F32),
            pltpu.VMEM((owners, 2 * owners, toks), F32),
            pltpu.VMEM((2, SIDE, 2 * SIDE * cap, toks), BF),
            pltpu.VMEM((2, 2, SIDE, toks, half_w), BF),
            pltpu.VMEM((2, 2, 2, SIDE, SIDE, cap, half_w), BF),
            pltpu.VMEM((2, 2, 2, SIDE, SIDE, cap, half_w), BF),
            pltpu.VMEM((2, width, hidden), BF),
            pltpu.VMEM((2, width, hidden), BF),
            pltpu.VMEM((2, 128, 2, hidden), BF),
            pltpu.VMEM((2, rows, toks), F32),
            pltpu.VMEM((2, rows, hidden), F32),
            pltpu.VMEM((2, 2, rows, hidden), BF),
            pltpu.VMEM((2, 2, SIDE - 1, toks, half_w), BF),
            pltpu.VMEM((2, 2, SIDE, cap, half_w), BF),
            pltpu.VMEM((2, SIDE, n_rows, 2 * hidden), BF),
            pltpu.VMEM((2, n_rows, 2 * hidden), BF),
            pltpu.VMEM((2, n_rows, 2 * hidden), BF),
            DMA((2, 4)), DMA((2, 4)),
            DMA((2, 2, 4)), DMA((2, 2, 4)),
            DMA((2, 2, 2, 4)), DMA((2, 2, 2, 4)),
            DMA((2,)),
            DMA((2, 2, 2, 4)), DMA((2, 2, 2, 4)), DMA((2, 2, 2)),
            DMA((2, 2, 4)), DMA((2, 2, 4)), DMA((2,)),
            DMA((2, 4)), DMA((2, 4)), DMA((2, 4)), DMA((2, 4)), DMA((2,)), DMA((2,)),
        ],
        compiler_params=pltpu.CompilerParams(
            collective_id=0, has_side_effects=True, vmem_limit_bytes=62 << 20
        ),
    )(route, tokens, out_grad, w_up, w_down)

    spread = lax.all_to_all(
        first_grad.reshape(owners, n_rows // owners, 2 * hidden), "expert", split_axis=0, concat_axis=0, tiled=True
    )
    choose = (partner[:, None] == jnp.arange(owners, dtype=jnp.int32)[None, :]).astype(BF)
    ordered = lax.dot_general(
        choose, spread, (((1,), (0,)), ((), ())), preferred_element_type=F32
    ).astype(BF)
    moved = lax.all_to_all(ordered, "expert", split_axis=0, concat_axis=0, tiled=True).reshape(n_rows, 2 * hidden)
    grad_up = jnp.stack([moved[:, :hidden], second_grad[:, :hidden]], axis=1)
    grad_down = jnp.stack([moved[:, hidden:], second_grad[:, hidden:]], axis=1)
    return (output, input_grad, grad_up, grad_down)


def solution(mesh):
    return jax.shard_map(
        body,
        mesh=mesh,
        in_specs=(
            P(("dp", "expert"), None),
            P(("dp", "expert"), None),
            P(("dp", "expert"), None),
            P(),
            P(None, "expert", None),
            P(None, "expert", None),
            P(("dp", "expert"), None),
        ),
        out_specs=(
            P(("dp", "expert"), None),
            P(("dp", "expert"), None),
            P("dp", "expert", None),
            P("dp", "expert", None),
        ),
        check_vma=False,
    )
```

```python
import functools

import jax
import jax.numpy as jnp
from jax import lax
from jax.experimental import pallas as pl
from jax.experimental.pallas import tpu as pltpu
from jax.sharding import PartitionSpec as P

MESH = pl.DeviceIdType.MESH
BF = jnp.bfloat16
F32 = jnp.float32
DMA = pltpu.SemaphoreType.DMA
SIDE = 4


class Place:
    def __init__(self):
        self.dp = lax.axis_index("dp")
        self.me = lax.axis_index("expert")
        self.y = self.me // SIDE
        self.x = lax.rem(self.me, SIDE)
        self.z = self.dp // 2
        self.core = lax.rem(self.dp, 2)

    def along_y(self, step):
        return (self.dp, lax.rem(self.y + step, SIDE) * SIDE + self.x)

    def along_x(self, step):
        return (self.dp, self.y * SIDE + lax.rem(self.x + step, SIDE))

    def first(self, half, step):
        return self.along_y(step) if half == 0 else self.along_x(step)

    def second(self, half, step):
        return self.along_x(step) if half == 0 else self.along_y(step)

    def first_at(self, half):
        return self.y if half == 0 else self.x

    def second_at(self, half):
        return self.x if half == 0 else self.y

    def along_z(self, step):
        return (lax.rem(self.z + step, SIDE) * 2 + self.core, self.me)

    def other_core(self):
        return (self.z * 2 + 1 - self.core, self.me)

    def greet(self):
        barrier = pltpu.get_barrier_semaphore()
        peers = [self.other_core()]
        for step in (1, 2, 3):
            peers += [self.along_y(step), self.along_x(step), self.along_z(step)]
        for peer in peers:
            pl.semaphore_signal(barrier, inc=1, device_id=peer, device_id_type=MESH)
        pl.semaphore_wait(barrier, len(peers))


def send(src, dst, send_sem, recv_sem, peer):
    copy = pltpu.make_async_remote_copy(
        src_ref=src, dst_ref=dst, send_sem=send_sem, recv_sem=recv_sem, device_id=peer, device_id_type=MESH
    )
    copy.start()
    return copy


def dot(a, b, over_a=1, over_b=0):
    return lax.dot_general(a, b, (((over_a,), (over_b,)), ((), ())), preferred_element_type=F32)


def kernel(
    cap, chosen, scale,
    partner, route, tok, og, wu_hbm, wd_hbm,
    out, ig, moved, g1_hbm, rec, cr, zr, ra, re,
    rt, rank, wt, pick, p1, st, xg, wu, wd, wbuf, wcol, slope, right, part, rbuf, own, xs, ld, fin, rb, rd,
    rt_s, rt_r, p1_s, p1_r, p2_s, p2_r, w_sem, r1_s, r1_r, own_sem, r2_s, r2_r, rb_sem,
    c_s, c_r, z_s, z_r, ld_sem, g_sem, m_s, m_r, mo_sem,
):
    at = Place()
    x, y, me = at.x, at.y, at.me
    toks = tok.shape[0]
    half_w = tok.shape[1] // 2
    hidden = wu.shape[2]
    rows = SIDE * SIDE * cap
    chunk = wbuf.shape[1]
    steps = (1, 2, 3)

    at.greet()
    rt[x * SIDE + y] = route[...]
    sends = []
    first = [
        send(route, rt.at[x * SIDE + y], rt_s.at[0, k], rt_r.at[0, k], at.along_y(k)) for k in steps
    ]

    def phase1(t):
        src = (tok, og)[t]
        out = []
        for h in (0, 1):
            for k in steps:
                out.append(
                    send(
                        src.at[:, pl.ds(h * half_w, half_w)],
                        p1.at[t, h, at.first_at(h)],
                        p1_s.at[t, h, k], p1_r.at[t, h, k], at.first(h, k),
                    )
                )
        return out

    def own1(t):
        src = (tok, og)[t]
        for h in (0, 1):
            p1[t, h, at.first_at(h)] = src[:, h * half_w : (h + 1) * half_w]

    arriving = [phase1(0), None]
    own1(0)
    for c in first:
        c.wait()
    block = rt.at[pl.ds(x * SIDE, SIDE)]
    second = [send(block, block, rt_s.at[1, k], rt_r.at[1, k], at.along_x(k)) for k in steps]

    def weights(hbm, vmem, lo, hi):
        def fetch(i):
            slot = lax.rem(i, 2)
            return pltpu.make_async_copy(
                hbm.at[pl.ds(pl.multiple_of(i * chunk, chunk), chunk)], wbuf.at[slot], w_sem.at[slot]
            )

        fetch(lo).start()

        def turn(i, carry):
            @pl.when(i + 1 < hi)
            def _():
                fetch(i + 1).start()

            fetch(i).wait()
            vmem[:, pl.ds(pl.multiple_of(i * chunk, chunk), chunk), :] = jnp.swapaxes(
                wbuf[lax.rem(i, 2)], 0, 1
            )
            return carry

        lax.fori_loop(lo, hi, turn, 0)

    n_chunks = wu.shape[1] // chunk
    for c in second:
        c.wait()

    before = (
        lax.broadcasted_iota(jnp.int32, (toks, toks), 0) < lax.broadcasted_iota(jnp.int32, (toks, toks), 1)
    ).astype(F32).astype(BF)
    n_exp = rank.shape[1]
    owners = n_exp // 2
    line = lax.broadcasted_iota(jnp.int32, (n_exp, toks), 0)
    expert = (lax.rem(line, owners) * 2 + line // owners).astype(F32)

    def ranks(n, carry):
        r = rt[n]
        named = jnp.zeros((n_exp, toks), F32)
        weight = jnp.zeros((n_exp, toks), F32)
        for k in range(chosen):
            m = (r[k : k + 1, :] == expert).astype(F32)
            named += m
            weight += m * r[8 + k : 9 + k, :]
        pos = dot(named.astype(BF), before)
        rank[n] = jnp.where(named > 0, pos, -1.0)
        wt[n] = weight
        return carry

    lax.fori_loop(0, SIDE * SIDE, ranks, 0)
    place = lax.broadcasted_iota(jnp.int32, (cap, toks), 0).astype(F32)

    def picks(j, carry):
        for h in (0, 1):
            n = x * SIDE + j if h == 0 else j * SIDE + y
            for s in (0, 1):
                for d in range(SIDE):
                    owner = y * SIDE + d if h == 0 else d * SIDE + x
                    q = rank[n, pl.ds(s * owners + owner, 1), :]
                    pick[h, j, (s * SIDE + d) * cap : (s * SIDE + d + 1) * cap, :] = (
                        (place == q).astype(F32).astype(BF)
                    )
        return carry

    lax.fori_loop(0, SIDE, picks, 0)

    def slot_weights(n, carry):
        for s in (0, 1):
            q = rank[n, pl.ds(s * owners + me, 1), :]
            w = wt[n, pl.ds(s * owners + me, 1), :]
            col = jnp.sum(jnp.where(place == q, w, 0.0), axis=1, keepdims=True)
            row = (lax.rem(n, SIDE) * SIDE + n // SIDE) * cap
            wcol[s, pl.ds(pl.multiple_of(row, cap), cap), :] = jnp.broadcast_to(col, (cap, toks))
        return carry

    lax.fori_loop(0, SIDE * SIDE, slot_weights, 0)

    weights(wu_hbm, wu, 0, n_chunks // 4)
    arriving[1] = phase1(1)
    own1(1)
    weights(wu_hbm, wu, n_chunks // 4, n_chunks)

    def stage(t):
        for h in (0, 1):
            mine = at.second_at(h)

            def turn(j, carry):
                got = dot(pick[h, j], p1[t, h, j]).astype(BF).reshape(2, SIDE, cap, half_w)
                st[t, h, :, :, j] = got
                return carry

            lax.fori_loop(0, SIDE, turn, 0)
            for s in (0, 1):
                own = st[t, h, s, pl.ds(mine, 1)].reshape(SIDE, cap, half_w)
                if h == 0:
                    xg[t, s, h, :, pl.ds(x, 1)] = own.reshape(SIDE, 1, cap, half_w)
                else:
                    xg[t, s, h, pl.ds(y, 1)] = own.reshape(1, SIDE, cap, half_w)

    def phase2(t, s):
        out = []
        for h in (0, 1):
            for k in steps:
                peer_at = lax.rem(at.second_at(h) + k, SIDE)
                dst = xg.at[t, s, h, :, x] if h == 0 else xg.at[t, s, h, y]
                out.append(
                    send(st.at[t, h, s, peer_at], dst, p2_s.at[t, s, h, k], p2_r.at[t, s, h, k], at.second(h, k))
                )
        return out

    moving = {}
    for c in arriving[0]:
        c.wait_recv()
    stage(0)
    moving[0, 0] = phase2(0, 0)
    weights(wd_hbm, wd, 0, n_chunks // 2)
    for c in arriving[1]:
        c.wait_recv()
    stage(1)
    moving[1, 0] = phase2(1, 0)
    weights(wd_hbm, wd, n_chunks // 2, n_chunks)

    tile = 256
    h_tiles = hidden // tile
    d_tiles = 2 * half_w // tile
    per_half = half_w // tile

    def inputs(t, s, h):
        return xg[t, s, h].reshape(rows, half_w)

    def put(i, got, dst):
        cols = pl.ds(pl.multiple_of(lax.rem(i, per_half) * tile, tile), tile)
        dst[i // per_half, :, :, :, cols] = got.astype(BF).reshape(SIDE, SIDE, cap, tile)

    def forward(s):
        def turn(n, carry):
            cols = pl.ds(pl.multiple_of(n * tile, tile), tile)
            pre = dot(inputs(0, s, 0), wu[s, 0:half_w, cols]) + dot(inputs(0, s, 1), wu[s, half_w : 2 * half_w, cols])
            w = wcol[s, :, 0:1]
            sig = 1.0 / (1.0 + jnp.exp(-pre))
            right[1, s, :, cols] = (pre * sig * w).astype(BF)
            slope[s, :, cols] = sig * (1.0 + pre * (1.0 - sig)) * w
            return carry

        lax.fori_loop(0, h_tiles, turn, 0)
        for c in moving[0, s]:
            c.wait_send()

        def result(i, carry):
            put(i, dot(right[1, s], wd[s, pl.ds(pl.multiple_of(i * tile, tile), tile), :], 1, 1), st.at[0, :, s])
            return carry

        lax.fori_loop(0, d_tiles, result, 0)

    def core_copy(s, n, zz):
        return pltpu.make_async_remote_copy(
            src_ref=xs.at[n % 2], dst_ref=cr.at[s, zz], send_sem=c_s.at[s, n], recv_sem=c_r.at[s, n],
            device_id=at.other_core(), device_id_type=MESH,
        )

    def gradient_tile(s, i, dst):
        cols = pl.ds(pl.multiple_of(lax.rem(i, per_half) * tile, tile), tile)

        def turn(t, carry):
            left = xg[t, s, i // per_half, :, :, :, cols].reshape(rows, tile)
            got = dot(left, right[t, s], 0, 0) * scale
            dst[:, pl.ds(pl.multiple_of(t * hidden, 128), hidden)] = got.astype(BF)
            return carry

        lax.fori_loop(0, 2, turn, 0)

    quarters = (2, 1, 3, 0)
    z_moving = {0: [], 1: []}

    def pair_sum(s, n):
        step = quarters[n]
        zz = lax.rem(at.z + step, SIDE)
        own[s, zz] = (own[s, zz].astype(F32) + ld[n % 2].astype(F32)).astype(BF)
        if step:
            z_moving[s].append(
                send(own.at[s, zz], zr.at[s, step - 1], z_s.at[s, step], z_r.at[s, step], at.along_z(step))
            )

    def fetch_pair(s, n):
        zz = lax.rem(at.z + quarters[n], SIDE)
        core_copy(s, n, zz).wait_recv()
        copy = pltpu.make_async_copy(cr.at[s, zz], ld.at[n % 2], ld_sem.at[n % 2])
        copy.start()
        return copy

    def backward(s):
        def turn(n, carry):
            cols = pl.ds(pl.multiple_of(n * tile, tile), tile)
            ga = dot(inputs(1, s, 0), wd[s, 0:half_w, cols]) + dot(inputs(1, s, 1), wd[s, half_w : 2 * half_w, cols])
            right[0, s, :, cols] = (ga * slope[s, :, cols]).astype(BF)
            return carry

        lax.fori_loop(0, h_tiles, turn, 0)
        for n, step in enumerate(quarters):
            zz = lax.rem(at.z + step, SIDE)
            if n >= 2:
                core_copy(s, n - 2, zz).wait_send()
            gradient_tile(s, zz * 2 + 1 - at.core, xs.at[n % 2])
            core_copy(s, n, zz).start()
            if n:
                got = fetch_pair(s, n - 1)
            gradient_tile(s, zz * 2 + at.core, own.at[s, zz])
            if n:
                got.wait()
                pair_sum(s, n - 1)

        def grad(i, carry):
            put(i, dot(right[0, s], wu[s, pl.ds(pl.multiple_of(i * tile, tile), tile), :], 1, 1), xg.at[1, s])
            return carry

        lax.fori_loop(0, d_tiles, grad, 0)
        fetch_pair(s, 3).wait()
        pair_sum(s, 3)
        for n in (2, 3):
            core_copy(s, n, 0).wait_send()

    def result_rows(t, s, h, other):
        block = st.at[0, h, s] if t == 0 else xg.at[1, s, h]
        return block.at[:, other] if h == 0 else block.at[other]

    def return1(t, s):
        copies = []
        for h in (0, 1):
            mine = at.second_at(h)
            dst = rec.at[t, h, :, s, mine]
            kept = pltpu.make_async_copy(result_rows(t, s, h, mine), dst, own_sem.at[t, s, h])
            kept.start()
            for k in steps:
                peer_at = lax.rem(mine + k, SIDE)
                copies.append(
                    send(result_rows(t, s, h, peer_at), dst, r1_s.at[t, s, h, k], r1_r.at[t, s, h, k], at.second(h, k))
                )
            copies.append(kept)
        return copies

    returning = {}
    for c in moving[0, 0]:
        c.wait_recv()
    moving[0, 1] = phase2(0, 1)
    forward(0)
    for c in moving[1, 0]:
        c.wait_recv()
    moving[1, 1] = phase2(1, 1)
    returning[0, 0] = return1(0, 0)
    backward(0)
    returning[1, 0] = return1(1, 0)
    for c in moving[0, 1]:
        c.wait_recv()
    forward(1)
    returning[0, 1] = return1(0, 1)
    for c in moving[1, 1]:
        c.wait_recv()
    backward(1)
    returning[1, 1] = return1(1, 1)

    def arrived(copies):
        for c in copies:
            if c.is_remote:
                c.wait_recv()
            else:
                c.wait()

    last = {0: [], 1: []}

    def return2(t, h):
        items = [(h, k) for k in (2, 1, 3, 0)]

        def fetch(n):
            h, k = items[n]
            copy = pltpu.make_async_copy(
                rec.at[t, h, lax.rem(at.first_at(h) + k, SIDE)], rbuf.at[n % 2], rb_sem.at[n % 2]
            )
            copy.start()
            return copy

        ahead = fetch(0)
        for n, (h, k) in enumerate(items):
            ahead.wait()
            if n + 1 < len(items):
                ahead = fetch(n + 1)
            j = lax.rem(at.first_at(h) + k, SIDE)
            got = dot(pick[h, j], rbuf[n % 2].reshape(2 * SIDE * cap, half_w), 0, 0)
            p1[t, h, k] = got.astype(BF)
            if k:
                last[t].append(
                    send(p1.at[t, h, k], part.at[t, h, k - 1], r2_s.at[t, h, k], r2_r.at[t, h, k], at.first(h, k))
                )

    def finish(t):
        result = (out, ig)[t]
        for c in last[t]:
            c.wait_recv()
        for h in (0, 1):
            total = p1[t, h, 0].astype(F32)
            for k in steps:
                total = total + part[t, h, k - 1].astype(F32)
            result[:, h * half_w : (h + 1) * half_w] = total.astype(BF)

    def gradients(s):
        total = own[s, at.z].astype(F32)
        for k in steps:
            z_moving[s][(2, 1, 3).index(k)].wait_recv()
            copy = pltpu.make_async_copy(zr.at[s, k - 1], ld.at[k % 2], ld_sem.at[k % 2])
            copy.start()
            copy.wait()
            total = total + ld[k % 2].astype(F32)
        return total.astype(BF)

    def exchange(number, src_of, dst_of, along):
        copies = []
        for u in (0, 1):
            use_x = along[u]
            mine = x if use_x else y
            kept = pltpu.make_async_copy(src_of(u, mine), dst_of(u, mine), mo_sem.at[number, u])
            kept.start()
            copies.append(kept)
            for k in steps:
                peer = at.along_x(k) if use_x else at.along_y(k)
                copies.append(
                    send(
                        src_of(u, lax.rem(mine + k, SIDE)), dst_of(u, mine),
                        m_s.at[number, u, k], m_r.at[number, u, k], peer,
                    )
                )
        return copies

    relocating = []

    def spread1():
        relocating.append(
            exchange(
                0, lambda u, o: fin.at[u, :, o] if u == 0 else fin.at[u, o], lambda u, m: ra.at[u, m], (True, False)
            )
        )

    def spread2():
        relocating.append(
            exchange(
                1,
                lambda u, o: ra.at[u, :, o],
                lambda u, m: rb.at[u, m] if u == 0 else rb.at[u, :, m],
                (False, True),
            )
        )

    def gather1():
        for i in range(SIDE * SIDE):
            for u in (0, 1):
                rd[u, i // SIDE, i % SIDE] = rb[u, partner[i] // SIDE, lax.rem(partner[i], SIDE)]
        relocating.append(
            exchange(
                2, lambda u, o: rd.at[u, o] if u == 0 else rd.at[u, :, o], lambda u, m: re.at[u, m], (False, True)
            )
        )

    def gather2():
        relocating.append(
            exchange(
                3,
                lambda u, o: re.at[u, :, o],
                lambda u, m: moved.at[u, :, m] if u == 0 else moved.at[u, m],
                (True, False),
            )
        )

    total = gradients(0)
    for u in (0, 1):
        fin[u] = total[:, u * hidden : (u + 1) * hidden].reshape(fin.shape[1:])
    spread1()
    arrived(returning[0, 0])
    arrived(returning[0, 1])
    return2(0, 0)
    arrived(relocating[0])
    spread2()
    return2(0, 1)
    arrived(relocating[1])
    gather1()
    arrived(returning[1, 0])
    arrived(returning[1, 1])
    return2(1, 0)
    arrived(relocating[2])
    gather2()
    return2(1, 1)
    finish(0)
    xs[1] = gradients(1)
    written = pltpu.make_async_copy(xs.at[1], g1_hbm, g_sem)
    written.start()
    finish(1)
    arrived(relocating[3])
    written.wait()
    for c in arriving[0] + arriving[1] + moving[1, 0] + moving[1, 1]:
        c.wait_send()
    for copies in list(returning.values()) + list(last.values()) + list(z_moving.values()) + relocating:
        for c in copies:
            if c.is_remote:
                c.wait_send()


def body(tokens, expert_ids, combine_weight, partner, w_up, w_down, out_grad):
    toks, chosen = expert_ids.shape
    width = tokens.shape[1]
    half_w = width // 2
    hidden = w_up.shape[2]
    owners = SIDE * SIDE
    cap = toks * chosen * 4 // (3 * 2 * owners)
    rows = owners * cap
    pad = jnp.zeros((8 - chosen, toks), F32)
    route = jnp.concatenate([expert_ids.T.astype(F32), pad, combine_weight.T, pad], axis=0)
    any_ = pl.BlockSpec(memory_space=pl.ANY)
    vmem = pl.BlockSpec(memory_space=pltpu.VMEM)
    n_rows = width // (2 * SIDE)
    piece = n_rows // owners
    output, input_grad, moved, second_grad, *_ = pl.pallas_call(
        functools.partial(kernel, cap, chosen, 1.0 / toks),
        out_shape=(
            jax.ShapeDtypeStruct((toks, width), BF),
            jax.ShapeDtypeStruct((toks, width), BF),
            jax.ShapeDtypeStruct((2, SIDE, SIDE, piece, hidden), BF),
            jax.ShapeDtypeStruct((n_rows, 2 * hidden), BF),
            jax.ShapeDtypeStruct((2, 2, SIDE, 2, SIDE, cap, half_w), BF),
            jax.ShapeDtypeStruct((2, SIDE, n_rows, 2 * hidden), BF),
            jax.ShapeDtypeStruct((2, SIDE - 1, n_rows, 2 * hidden), BF),
            jax.ShapeDtypeStruct((2, SIDE, SIDE, piece, hidden), BF),
            jax.ShapeDtypeStruct((2, SIDE, SIDE, piece, hidden), BF),
        ),
        in_specs=[pl.BlockSpec(memory_space=pltpu.SMEM), vmem, vmem, vmem, any_, any_],
        out_specs=(vmem, vmem, any_, any_, any_, any_, any_, any_, any_),
        scratch_shapes=[
            pltpu.VMEM((owners, 16, toks), F32),
            pltpu.VMEM((owners, 2 * owners, toks), F32),
            pltpu.VMEM((owners, 2 * owners, toks), F32),
            pltpu.VMEM((2, SIDE, 2 * SIDE * cap, toks), BF),
            pltpu.VMEM((2, 2, SIDE, toks, half_w), BF),
            pltpu.VMEM((2, 2, 2, SIDE, SIDE, cap, half_w), BF),
            pltpu.VMEM((2, 2, 2, SIDE, SIDE, cap, half_w), BF),
            pltpu.VMEM((2, width, hidden), BF),
            pltpu.VMEM((2, width, hidden), BF),
            pltpu.VMEM((2, 128, 2, hidden), BF),
            pltpu.VMEM((2, rows, toks), F32),
            pltpu.VMEM((2, rows, hidden), F32),
            pltpu.VMEM((2, 2, rows, hidden), BF),
            pltpu.VMEM((2, 2, SIDE - 1, toks, half_w), BF),
            pltpu.VMEM((2, 2, SIDE, cap, half_w), BF),
            pltpu.VMEM((2, SIDE, n_rows, 2 * hidden), BF),
            pltpu.VMEM((2, n_rows, 2 * hidden), BF),
            pltpu.VMEM((2, n_rows, 2 * hidden), BF),
            pltpu.VMEM((2, SIDE, SIDE, piece, hidden), BF),
            pltpu.VMEM((2, SIDE, SIDE, piece, hidden), BF),
            pltpu.VMEM((2, SIDE, SIDE, piece, hidden), BF),
            DMA((2, 4)), DMA((2, 4)),
            DMA((2, 2, 4)), DMA((2, 2, 4)),
            DMA((2, 2, 2, 4)), DMA((2, 2, 2, 4)),
            DMA((2,)),
            DMA((2, 2, 2, 4)), DMA((2, 2, 2, 4)), DMA((2, 2, 2)),
            DMA((2, 2, 4)), DMA((2, 2, 4)), DMA((2,)),
            DMA((2, 4)), DMA((2, 4)), DMA((2, 4)), DMA((2, 4)), DMA((2,)), DMA,
            DMA((4, 2, 4)), DMA((4, 2, 4)), DMA((4, 2)),
        ],
        compiler_params=pltpu.CompilerParams(
            collective_id=0, has_side_effects=True, vmem_limit_bytes=62 << 20
        ),
    )(partner, route, tokens, out_grad, w_up, w_down)

    moved = moved.reshape(2, n_rows, hidden)
    grad_up = jnp.stack([moved[0], second_grad[:, :hidden]], axis=1)
    grad_down = jnp.stack([moved[1], second_grad[:, hidden:]], axis=1)
    return (output, input_grad, grad_up, grad_down)


def solution(mesh):
    return jax.shard_map(
        body,
        mesh=mesh,
        in_specs=(
            P(("dp", "expert"), None),
            P(("dp", "expert"), None),
            P(("dp", "expert"), None),
            P(),
            P(None, "expert", None),
            P(None, "expert", None),
            P(("dp", "expert"), None),
        ),
        out_specs=(
            P(("dp", "expert"), None),
            P(("dp", "expert"), None),
            P("dp", "expert", None),
            P("dp", "expert", None),
        ),
        check_vma=False,
    )
```

```python
import functools

import jax
import jax.numpy as jnp
from jax import lax
from jax.experimental import pallas as pl
from jax.experimental.pallas import tpu as pltpu
from jax.sharding import PartitionSpec as P

MESH = pl.DeviceIdType.MESH
BF = jnp.bfloat16
F32 = jnp.float32
DMA = pltpu.SemaphoreType.DMA
SIDE = 4


class Place:
    def __init__(self):
        self.dp = lax.axis_index("dp")
        self.me = lax.axis_index("expert")
        self.y = self.me // SIDE
        self.x = lax.rem(self.me, SIDE)
        self.z = self.dp // 2
        self.core = lax.rem(self.dp, 2)

    def along_y(self, step):
        return (self.dp, lax.rem(self.y + step, SIDE) * SIDE + self.x)

    def along_x(self, step):
        return (self.dp, self.y * SIDE + lax.rem(self.x + step, SIDE))

    def first(self, half, step):
        return self.along_y(step) if half == 0 else self.along_x(step)

    def second(self, half, step):
        return self.along_x(step) if half == 0 else self.along_y(step)

    def first_at(self, half):
        return self.y if half == 0 else self.x

    def second_at(self, half):
        return self.x if half == 0 else self.y

    def along_z(self, step):
        return (lax.rem(self.z + step, SIDE) * 2 + self.core, self.me)

    def other_core(self):
        return (self.z * 2 + 1 - self.core, self.me)

    def greet(self):
        barrier = pltpu.get_barrier_semaphore()
        peers = [self.other_core()]
        for step in (1, 2, 3):
            peers += [self.along_y(step), self.along_x(step), self.along_z(step)]
        for peer in peers:
            pl.semaphore_signal(barrier, inc=1, device_id=peer, device_id_type=MESH)
        pl.semaphore_wait(barrier, len(peers))


def send(src, dst, send_sem, recv_sem, peer):
    copy = pltpu.make_async_remote_copy(
        src_ref=src, dst_ref=dst, send_sem=send_sem, recv_sem=recv_sem, device_id=peer, device_id_type=MESH
    )
    copy.start()
    return copy


def dot(a, b, over_a=1, over_b=0):
    return lax.dot_general(a, b, (((over_a,), (over_b,)), ((), ())), preferred_element_type=F32)


def kernel(
    cap, chosen, scale,
    partner, route, tok, og, wu_hbm, wd_hbm,
    out, ig, moved_up, moved_down, kept_up, kept_down, zr, ra, re,
    rt, rank, wt, pick, p1, st, xg, wu, wd, wbuf, wcol, slope, right, part, own, xs, ld, cr, fin, rb, rd,
    rt_s, rt_r, p1_s, p1_r, p1_o, p2_s, p2_r, w_sem, r1_s, r1_r, own_sem, r2_s, r2_r,
    c_s, c_r, z_s, z_r, ld_sem, g_sem, m_s, m_r, mo_sem, row_free, core_free,
):
    at = Place()
    x, y, me = at.x, at.y, at.me
    toks = tok.shape[0]
    half_w = tok.shape[1] // 2
    hidden = wu.shape[2]
    rows = SIDE * SIDE * cap
    chunk = wbuf.shape[1]
    steps = (1, 2, 3)

    at.greet()
    rt[x * SIDE + y] = route[...]
    first = [
        send(route, rt.at[x * SIDE + y], rt_s.at[0, k], rt_r.at[0, k], at.along_y(k)) for k in steps
    ]

    def arrived(copies):
        for c in copies:
            if c.is_remote:
                c.wait_recv()
            else:
                c.wait()

    def sent(copies):
        for c in copies:
            if c.is_remote:
                c.wait_send()

    def phase1(t):
        copies = []
        for h in (0, 1):
            block = (tok, og)[t].at[:, pl.ds(h * half_w, half_w)]
            dst = p1.at[t, h, at.first_at(h)]
            for k in steps:
                copies.append(send(block, dst, p1_s.at[t, h, k], p1_r.at[t, h, k], at.first(h, k)))
            kept = pltpu.make_async_copy(block, dst, p1_o.at[t, h])
            kept.start()
            copies.append(kept)
        return copies

    arriving = [phase1(0), None]

    def weights(hbm, vmem, lo, hi):
        def fetch(i):
            slot = lax.rem(i, 2)
            return pltpu.make_async_copy(
                hbm.at[pl.ds(pl.multiple_of(i * chunk, chunk), chunk)], wbuf.at[slot], w_sem.at[slot]
            )

        fetch(lo).start()

        def turn(i, carry):
            @pl.when(i + 1 < hi)
            def _():
                fetch(i + 1).start()

            fetch(i).wait()
            vmem[:, pl.ds(pl.multiple_of(i * chunk, chunk), chunk), :] = jnp.swapaxes(
                wbuf[lax.rem(i, 2)], 0, 1
            )
            return carry

        lax.fori_loop(lo, hi, turn, 0)

    for c in first:
        c.wait()
    block = rt.at[pl.ds(x * SIDE, SIDE)]
    second = [send(block, block, rt_s.at[1, k], rt_r.at[1, k], at.along_x(k)) for k in steps]
    n_chunks = wu.shape[1] // chunk
    weights(wu_hbm, wu, 0, n_chunks // 4)
    for c in second:
        c.wait()

    before = (
        lax.broadcasted_iota(jnp.int32, (toks, toks), 0) < lax.broadcasted_iota(jnp.int32, (toks, toks), 1)
    ).astype(F32).astype(BF)
    n_exp = rank.shape[1]
    owners = n_exp // 2
    line = lax.broadcasted_iota(jnp.int32, (n_exp, toks), 0)
    expert = (lax.rem(line, owners) * 2 + line // owners).astype(F32)

    def ranks(n, carry):
        r = rt[n]
        named = jnp.zeros((n_exp, toks), F32)
        weight = jnp.zeros((n_exp, toks), F32)
        for k in range(chosen):
            m = (r[k : k + 1, :] == expert).astype(F32)
            named += m
            weight += m * r[8 + k : 9 + k, :]
        pos = dot(named.astype(BF), before)
        rank[n] = jnp.where(named > 0, pos, -1.0)
        wt[n] = weight
        return carry

    lax.fori_loop(0, SIDE * SIDE, ranks, 0)
    place = lax.broadcasted_iota(jnp.int32, (cap, toks), 0).astype(F32)

    def picks(j, carry):
        for h in (0, 1):
            n = x * SIDE + j if h == 0 else j * SIDE + y
            for s in (0, 1):
                for d in range(SIDE):
                    owner = y * SIDE + d if h == 0 else d * SIDE + x
                    q = rank[n, pl.ds(s * owners + owner, 1), :]
                    pick[h, j, (s * SIDE + d) * cap : (s * SIDE + d + 1) * cap, :] = (
                        (place == q).astype(F32).astype(BF)
                    )
        return carry

    lax.fori_loop(0, SIDE, picks, 0)

    def slot_weights(n, carry):
        for s in (0, 1):
            q = rank[n, pl.ds(s * owners + me, 1), :]
            w = wt[n, pl.ds(s * owners + me, 1), :]
            col = jnp.sum(jnp.where(place == q, w, 0.0), axis=1, keepdims=True)
            row = (lax.rem(n, SIDE) * SIDE + n // SIDE) * cap
            wcol[s, pl.ds(pl.multiple_of(row, cap), cap), :] = jnp.broadcast_to(col, (cap, toks))
        return carry

    lax.fori_loop(0, SIDE * SIDE, slot_weights, 0)

    arriving[1] = phase1(1)
    weights(wu_hbm, wu, n_chunks // 4, n_chunks)

    def stage(t):
        for h in (0, 1):
            mine = at.second_at(h)

            def turn(j, carry):
                got = dot(pick[h, j], p1[t, h, j]).astype(BF).reshape(2, SIDE, cap, half_w)
                st[t, h, :, :, j] = got
                return carry

            lax.fori_loop(0, SIDE, turn, 0)
            for s in (0, 1):
                own = st[t, h, s, pl.ds(mine, 1)].reshape(SIDE, cap, half_w)
                if h == 0:
                    xg[t, s, h, :, pl.ds(x, 1)] = own.reshape(SIDE, 1, cap, half_w)
                else:
                    xg[t, s, h, pl.ds(y, 1)] = own.reshape(1, SIDE, cap, half_w)

    def phase2(t, s):
        out = []
        for h in (0, 1):
            for k in steps:
                peer_at = lax.rem(at.second_at(h) + k, SIDE)
                dst = xg.at[t, s, h, :, x] if h == 0 else xg.at[t, s, h, y]
                out.append(
                    send(st.at[t, h, s, peer_at], dst, p2_s.at[t, s, h, k], p2_r.at[t, s, h, k], at.second(h, k))
                )
        return out

    moving = {}
    arrived(arriving[0])
    stage(0)
    moving[0, 0] = phase2(0, 0)
    weights(wd_hbm, wd, 0, n_chunks // 2)
    arrived(arriving[1])
    stage(1)
    moving[1, 0] = phase2(1, 0)
    weights(wd_hbm, wd, n_chunks // 2, n_chunks)

    tile = 256
    h_tiles = hidden // tile
    d_tiles = 2 * half_w // tile
    per_half = half_w // tile

    def inputs(t, s, h):
        return xg[t, s, h].reshape(rows, half_w)

    def put(i, got, dst):
        cols = pl.ds(pl.multiple_of(lax.rem(i, per_half) * tile, tile), tile)
        dst[i // per_half, :, :, :, cols] = got.astype(BF).reshape(SIDE, SIDE, cap, tile)

    def forward(s):
        def turn(n, carry):
            cols = pl.ds(pl.multiple_of(n * tile, tile), tile)
            pre = dot(inputs(0, s, 0), wu[s, 0:half_w, cols]) + dot(inputs(0, s, 1), wu[s, half_w : 2 * half_w, cols])
            w = wcol[s, :, 0:1]
            sig = 1.0 / (1.0 + jnp.exp(-pre))
            right[1, s, :, cols] = (pre * sig * w).astype(BF)
            slope[s, :, cols] = sig * (1.0 + pre * (1.0 - sig)) * w
            return carry

        lax.fori_loop(0, h_tiles, turn, 0)
        sent(moving[0, s])

        def result(i, carry):
            put(i, dot(right[1, s], wd[s, pl.ds(pl.multiple_of(i * tile, tile), tile), :], 1, 1), st.at[0, :, s])
            return carry

        lax.fori_loop(0, d_tiles, result, 0)

    def core_copy(s, n):
        return pltpu.make_async_remote_copy(
            src_ref=xs.at[n % 2], dst_ref=cr.at[n], send_sem=c_s.at[s, n], recv_sem=c_r.at[s, n],
            device_id=at.other_core(), device_id_type=MESH,
        )

    def release_rows(t, s):
        for k in steps:
            for peer in (at.along_x(k), at.along_y(k)):
                pl.semaphore_signal(row_free.at[t, s], inc=1, device_id=peer, device_id_type=MESH)

    def gradient_tile(s, i, dst):
        cols = pl.ds(pl.multiple_of(lax.rem(i, per_half) * tile, tile), tile)

        def turn(t, carry):
            left = xg[t, s, i // per_half, :, :, :, cols].reshape(rows, tile)
            got = dot(left, right[t, s], 0, 0) * scale
            dst[:, pl.ds(pl.multiple_of(t * hidden, 128), hidden)] = got.astype(BF)
            return carry

        lax.fori_loop(0, 2, turn, 0)

    quarters = (2, 1, 3, 0)
    z_moving = {0: [], 1: []}

    def pair_sum(s, n):
        core_copy(s, n).wait_recv()
        step = quarters[n]
        zz = lax.rem(at.z + step, SIDE)
        own[s, zz] = (own[s, zz].astype(F32) + cr[n].astype(F32)).astype(BF)
        if step:
            z_moving[s].append(
                send(own.at[s, zz], zr.at[s, step - 1], z_s.at[s, step], z_r.at[s, step], at.along_z(step))
            )

    def backward(s):
        def turn(n, carry):
            cols = pl.ds(pl.multiple_of(n * tile, tile), tile)
            ga = dot(inputs(1, s, 0), wd[s, 0:half_w, cols]) + dot(inputs(1, s, 1), wd[s, half_w : 2 * half_w, cols])
            right[0, s, :, cols] = (ga * slope[s, :, cols]).astype(BF)
            return carry

        lax.fori_loop(0, h_tiles, turn, 0)
        if s:
            pl.semaphore_wait(core_free, 1)
        for n, step in enumerate(quarters):
            zz = lax.rem(at.z + step, SIDE)
            if n >= 2:
                core_copy(s, n - 2).wait_send()
            gradient_tile(s, zz * 2 + 1 - at.core, xs.at[n % 2])
            core_copy(s, n).start()
            gradient_tile(s, zz * 2 + at.core, own.at[s, zz])
            if n:
                pair_sum(s, n - 1)
        release_rows(1, s)

        def grad(i, carry):
            put(i, dot(right[0, s], wu[s, pl.ds(pl.multiple_of(i * tile, tile), tile), :], 1, 1), xg.at[1, s])
            return carry

        lax.fori_loop(0, d_tiles, grad, 0)
        pair_sum(s, 3)
        if s == 0:
            pl.semaphore_signal(core_free, inc=1, device_id=at.other_core(), device_id_type=MESH)
        for n in (2, 3):
            core_copy(s, n).wait_send()

    def result_rows(t, s, h, other):
        block = st.at[0, h, s] if t == 0 else xg.at[1, s, h]
        return block.at[:, other] if h == 0 else block.at[other]

    def home(t, s, h):
        return st.at[1, h, s] if t == 0 else xg.at[0, s, h]

    def return1(t, s):
        pl.semaphore_wait(row_free.at[t, s], 6)
        copies = []
        for h in (0, 1):
            mine = at.second_at(h)
            dst = home(t, s, h).at[mine]
            kept = pltpu.make_async_copy(result_rows(t, s, h, mine), dst, own_sem.at[t, s, h])
            kept.start()
            for k in steps:
                peer_at = lax.rem(mine + k, SIDE)
                copies.append(
                    send(result_rows(t, s, h, peer_at), dst, r1_s.at[t, s, h, k], r1_r.at[t, s, h, k], at.second(h, k))
                )
            copies.append(kept)
        return copies

    returning = {}
    arrived(moving[0, 0])
    moving[0, 1] = phase2(0, 1)
    forward(0)
    arrived(moving[1, 0])
    moving[1, 1] = phase2(1, 1)
    sent(moving[1, 0])
    release_rows(0, 0)
    backward(0)
    returning[0, 0] = return1(0, 0)
    returning[1, 0] = return1(1, 0)
    arrived(moving[0, 1])
    forward(1)
    arrived(moving[1, 1])
    sent(moving[1, 1])
    release_rows(0, 1)
    returning[0, 1] = return1(0, 1)
    backward(1)
    returning[1, 1] = return1(1, 1)

    last = {0: [], 1: []}

    def return2(t, h):
        for k in (2, 1, 3, 0):
            j = lax.rem(at.first_at(h) + k, SIDE)
            came = [home(t, s, h)[:, j].reshape(SIDE * cap, half_w) for s in (0, 1)]
            got = dot(pick[h, j], jnp.concatenate(came, axis=0), 0, 0)
            p1[t, h, k] = got.astype(BF)
            if k:
                last[t].append(
                    send(p1.at[t, h, k], part.at[t, h, k - 1], r2_s.at[t, h, k], r2_r.at[t, h, k], at.first(h, k))
                )

    def finish(t):
        result = (out, ig)[t]
        for c in last[t]:
            c.wait_recv()
        for h in (0, 1):
            total = p1[t, h, 0].astype(F32)
            for k in steps:
                total = total + part[t, h, k - 1].astype(F32)
            result[:, h * half_w : (h + 1) * half_w] = total.astype(BF)

    def gradients(s, keep):
        room = (ld.at[0], ld.at[1], xs.at[0])
        copies = []
        for k in (1, 3, 2):
            z_moving[s][(2, 1, 3).index(k)].wait_recv()
            copy = pltpu.make_async_copy(zr.at[s, k - 1], room[k - 1], ld_sem.at[k - 1])
            copy.start()
            copies.append(copy)
        for copy in copies:
            copy.wait()

        def turn(r, carry):
            some = pl.ds(pl.multiple_of(r * 16, 16), 16)
            total = own[s, at.z, some].astype(F32)
            for buf in room:
                total = total + buf[some].astype(F32)
            keep(r, total.astype(BF))
            return carry

        lax.fori_loop(0, xs.shape[1] // 16, turn, 0)

    def exchange(number, src_of, dst_of, along):
        copies = []
        for u in (0, 1):
            use_x = along[u]
            mine = x if use_x else y
            kept = pltpu.make_async_copy(src_of(u, mine), dst_of(u, mine), mo_sem.at[number, u])
            kept.start()
            copies.append(kept)
            for k in steps:
                peer = at.along_x(k) if use_x else at.along_y(k)
                copies.append(
                    send(
                        src_of(u, lax.rem(mine + k, SIDE)), dst_of(u, mine),
                        m_s.at[number, u, k], m_r.at[number, u, k], peer,
                    )
                )
        return copies

    relocating = []

    def spread1():
        relocating.append(
            exchange(
                0, lambda u, o: fin.at[u, :, o] if u == 0 else fin.at[u, o], lambda u, m: ra.at[u, m], (True, False)
            )
        )

    def spread2():
        relocating.append(
            exchange(
                1,
                lambda u, o: ra.at[u, :, o],
                lambda u, m: rb.at[u, m] if u == 0 else rb.at[u, :, m],
                (False, True),
            )
        )

    def gather1():
        for i in range(SIDE * SIDE):
            for u in (0, 1):
                rd[u, i // SIDE, i % SIDE] = rb[u, partner[i] // SIDE, lax.rem(partner[i], SIDE)]
        relocating.append(
            exchange(
                2, lambda u, o: rd.at[u, o] if u == 0 else rd.at[u, :, o], lambda u, m: re.at[u, m], (False, True)
            )
        )

    def gather2():
        relocating.append(
            exchange(
                3,
                lambda u, o: re.at[u, :, o],
                lambda u, m: moved_up.at[:, m] if u == 0 else moved_down.at[m],
                (True, False),
            )
        )

    def keep_first(r, total):
        for u in (0, 1):
            fin[u, r // SIDE, lax.rem(r, SIDE)] = total[:, u * hidden : (u + 1) * hidden]

    def keep_second(r, total):
        xs[1, pl.ds(pl.multiple_of(r * 16, 16), 16)] = total

    gradients(0, keep_first)
    spread1()
    arrived(returning[0, 0])
    arrived(returning[0, 1])
    return2(0, 0)
    arrived(relocating[0])
    spread2()
    return2(0, 1)
    arrived(relocating[1])
    gather1()
    arrived(returning[1, 0])
    arrived(returning[1, 1])
    return2(1, 0)
    arrived(relocating[2])
    gather2()
    return2(1, 1)
    finish(0)
    gradients(1, keep_second)
    written = []
    for u, dst in enumerate((kept_up, kept_down)):
        copy = pltpu.make_async_copy(xs.at[1, :, pl.ds(u * hidden, hidden)], dst, g_sem.at[u])
        copy.start()
        written.append(copy)
    finish(1)
    arrived(relocating[3])
    for c in written:
        c.wait()
    sent(arriving[0] + arriving[1])
    for copies in list(returning.values()) + list(last.values()) + list(z_moving.values()) + relocating:
        sent(copies)


def body(tokens, expert_ids, combine_weight, partner, w_up, w_down, out_grad):
    toks, chosen = expert_ids.shape
    width = tokens.shape[1]
    half_w = width // 2
    hidden = w_up.shape[2]
    owners = SIDE * SIDE
    cap = toks * chosen * 4 // (3 * 2 * owners)
    rows = owners * cap
    pad = jnp.zeros((8 - chosen, toks), F32)
    route = jnp.concatenate([expert_ids.T.astype(F32), pad, combine_weight.T, pad], axis=0)
    any_ = pl.BlockSpec(memory_space=pl.ANY)
    vmem = pl.BlockSpec(memory_space=pltpu.VMEM)
    n_rows = width // (2 * SIDE)
    piece = n_rows // owners
    tile_shape = jax.ShapeDtypeStruct((n_rows, hidden), BF)
    piece_shape = (SIDE, SIDE, piece, hidden)
    output, input_grad, moved_up, moved_down, kept_up, kept_down, *_ = pl.pallas_call(
        functools.partial(kernel, cap, chosen, 1.0 / toks),
        out_shape=(
            jax.ShapeDtypeStruct((toks, width), BF),
            jax.ShapeDtypeStruct((toks, width), BF),
            jax.ShapeDtypeStruct(piece_shape, BF),
            jax.ShapeDtypeStruct(piece_shape, BF),
            tile_shape,
            tile_shape,
            jax.ShapeDtypeStruct((2, SIDE - 1, n_rows, 2 * hidden), BF),
            jax.ShapeDtypeStruct((2, *piece_shape), BF),
            jax.ShapeDtypeStruct((2, *piece_shape), BF),
        ),
        in_specs=[pl.BlockSpec(memory_space=pltpu.SMEM), vmem, any_, any_, any_, any_],
        out_specs=(vmem, vmem, any_, any_, any_, any_, any_, any_, any_),
        scratch_shapes=[
            pltpu.VMEM((owners, 16, toks), F32),
            pltpu.VMEM((owners, 2 * owners, toks), F32),
            pltpu.VMEM((owners, 2 * owners, toks), F32),
            pltpu.VMEM((2, SIDE, 2 * SIDE * cap, toks), BF),
            pltpu.VMEM((2, 2, SIDE, toks, half_w), BF),
            pltpu.VMEM((2, 2, 2, SIDE, SIDE, cap, half_w), BF),
            pltpu.VMEM((2, 2, 2, SIDE, SIDE, cap, half_w), BF),
            pltpu.VMEM((2, width, hidden), BF),
            pltpu.VMEM((2, width, hidden), BF),
            pltpu.VMEM((2, 128, 2, hidden), BF),
            pltpu.VMEM((2, rows, toks), F32),
            pltpu.VMEM((2, rows, hidden), F32),
            pltpu.VMEM((2, 2, rows, hidden), BF),
            pltpu.VMEM((2, 2, SIDE - 1, toks, half_w), BF),
            pltpu.VMEM((2, SIDE, n_rows, 2 * hidden), BF),
            pltpu.VMEM((2, n_rows, 2 * hidden), BF),
            pltpu.VMEM((2, n_rows, 2 * hidden), BF),
            pltpu.VMEM((SIDE, n_rows, 2 * hidden), BF),
            pltpu.VMEM((2, *piece_shape), BF),
            pltpu.VMEM((2, *piece_shape), BF),
            pltpu.VMEM((2, *piece_shape), BF),
            DMA((2, 4)), DMA((2, 4)),
            DMA((2, 2, 4)), DMA((2, 2, 4)), DMA((2, 2)),
            DMA((2, 2, 2, 4)), DMA((2, 2, 2, 4)),
            DMA((2,)),
            DMA((2, 2, 2, 4)), DMA((2, 2, 2, 4)), DMA((2, 2, 2)),
            DMA((2, 2, 4)), DMA((2, 2, 4)),
            DMA((2, 4)), DMA((2, 4)), DMA((2, 4)), DMA((2, 4)), DMA((3,)), DMA((2,)),
            DMA((4, 2, 4)), DMA((4, 2, 4)), DMA((4, 2)),
            pltpu.SemaphoreType.REGULAR((2, 2)), pltpu.SemaphoreType.REGULAR,
        ],
        compiler_params=pltpu.CompilerParams(
            collective_id=0, has_side_effects=True, vmem_limit_bytes=62 << 20
        ),
    )(partner, route, tokens, out_grad, w_up, w_down)

    grad_up = jnp.stack([moved_up.reshape(n_rows, hidden), kept_up], axis=1)
    grad_down = jnp.stack([moved_down.reshape(n_rows, hidden), kept_down], axis=1)
    return (output, input_grad, grad_up, grad_down)


def solution(mesh):
    return jax.shard_map(
        body,
        mesh=mesh,
        in_specs=(
            P(("dp", "expert"), None),
            P(("dp", "expert"), None),
            P(("dp", "expert"), None),
            P(),
            P(None, "expert", None),
            P(None, "expert", None),
            P(("dp", "expert"), None),
        ),
        out_specs=(
            P(("dp", "expert"), None),
            P(("dp", "expert"), None),
            P("dp", "expert", None),
            P("dp", "expert", None),
        ),
        check_vma=False,
    )
```

```python
import functools

import jax
import jax.numpy as jnp
from jax import lax
from jax.experimental import pallas as pl
from jax.experimental.pallas import tpu as pltpu
from jax.sharding import PartitionSpec as P

MESH = pl.DeviceIdType.MESH
BF = jnp.bfloat16
F32 = jnp.float32
DMA = pltpu.SemaphoreType.DMA
SIDE = 4


class Place:
    def __init__(self):
        self.dp = lax.axis_index("dp")
        self.me = lax.axis_index("expert")
        self.y = self.me // SIDE
        self.x = lax.rem(self.me, SIDE)
        self.z = self.dp // 2
        self.core = lax.rem(self.dp, 2)

    def along_y(self, step):
        return (self.dp, lax.rem(self.y + step, SIDE) * SIDE + self.x)

    def along_x(self, step):
        return (self.dp, self.y * SIDE + lax.rem(self.x + step, SIDE))

    def first(self, half, step):
        return self.along_y(step) if half == 0 else self.along_x(step)

    def second(self, half, step):
        return self.along_x(step) if half == 0 else self.along_y(step)

    def first_at(self, half):
        return self.y if half == 0 else self.x

    def second_at(self, half):
        return self.x if half == 0 else self.y

    def along_z(self, step):
        return (lax.rem(self.z + step, SIDE) * 2 + self.core, self.me)

    def other_core(self):
        return (self.z * 2 + 1 - self.core, self.me)

    def greet(self):
        barrier = pltpu.get_barrier_semaphore()
        peers = [self.other_core()]
        for step in (1, 2, 3):
            peers += [self.along_y(step), self.along_x(step), self.along_z(step)]
        for peer in peers:
            pl.semaphore_signal(barrier, inc=1, device_id=peer, device_id_type=MESH)
        pl.semaphore_wait(barrier, len(peers))


def send(src, dst, send_sem, recv_sem, peer):
    copy = pltpu.make_async_remote_copy(
        src_ref=src, dst_ref=dst, send_sem=send_sem, recv_sem=recv_sem, device_id=peer, device_id_type=MESH
    )
    copy.start()
    return copy


def dot(a, b, over_a=1, over_b=0):
    return lax.dot_general(a, b, (((over_a,), (over_b,)), ((), ())), preferred_element_type=F32)


def kernel(
    cap, chosen, scale,
    partner, ids, gate, tok, og, wu_hbm, wd_hbm,
    out, ig, moved_up, moved_down, kept_up, kept_down, zr, ra, re,
    rt, rank, wt, pick, p1, st, xg, wu, wd, wbuf, wcol, slope, right, part, own, xs, ld, cr, fin, rb, rd,
    rt_s, rt_r, p1_s, p1_r, p1_o, p2_s, p2_r, w_sem, r1_s, r1_r, own_sem, r2_s, r2_r,
    c_s, c_r, z_s, z_r, ld_sem, g_sem, m_s, m_r, mo_sem, row_free, core_free,
):
    at = Place()
    x, y, me = at.x, at.y, at.me
    toks = tok.shape[0]
    half_w = tok.shape[1] // 2
    hidden = wu.shape[2]
    rows = SIDE * SIDE * cap
    chunk = wbuf.shape[1]
    steps = (1, 2, 3)

    at.greet()
    route = rt.at[x * SIDE + y]
    route[0:chosen] = ids[...].astype(F32)
    route[8 : 8 + chosen] = gate[...]
    first = [send(route, route, rt_s.at[0, k], rt_r.at[0, k], at.along_y(k)) for k in steps]

    def arrived(copies):
        for c in copies:
            if c.is_remote:
                c.wait_recv()
            else:
                c.wait()

    def sent(copies):
        for c in copies:
            if c.is_remote:
                c.wait_send()

    def phase1(t):
        copies = []
        for h in (0, 1):
            block = (tok, og)[t].at[:, pl.ds(h * half_w, half_w)]
            dst = p1.at[t, h, at.first_at(h)]
            for k in (1, 3):
                copies.append(send(block, dst, p1_s.at[t, h, k], p1_r.at[t, h, k], at.first(h, k)))
            kept = pltpu.make_async_copy(block, dst, p1_o.at[t, h])
            kept.start()
            copies.append(kept)
        return copies

    def forward1(t):
        copies = []
        part_rows = toks // 2
        for h in (0, 1):
            for k, sem in ((1, 2), (3, 0)):
                arriving[t][3 * h + k // 2].wait_recv()
                origin = lax.rem(at.first_at(h) + SIDE - k, SIDE)
                block = p1.at[t, h, origin, pl.ds((k // 2) * part_rows, part_rows)]
                copies.append(send(block, block, p1_s.at[t, h, sem], p1_r.at[t, h, sem], at.first(h, k)))
            arriving[t][3 * h + 2].wait()
        return copies

    def weights(hbm, vmem, lo, hi):
        def fetch(i):
            slot = lax.rem(i, 2)
            return pltpu.make_async_copy(
                hbm.at[pl.ds(pl.multiple_of(i * chunk, chunk), chunk)], wbuf.at[slot], w_sem.at[slot]
            )

        fetch(lo).start()

        def turn(i, carry):
            @pl.when(i + 1 < hi)
            def _():
                fetch(i + 1).start()

            fetch(i).wait()
            vmem[:, pl.ds(pl.multiple_of(i * chunk, chunk), chunk), :] = jnp.swapaxes(
                wbuf[lax.rem(i, 2)], 0, 1
            )
            return carry

        lax.fori_loop(lo, hi, turn, 0)

    for c in first:
        c.wait()
    block = rt.at[pl.ds(x * SIDE, SIDE)]
    second = [send(block, block, rt_s.at[1, k], rt_r.at[1, k], at.along_x(k)) for k in steps]
    arriving = [phase1(0)]
    n_chunks = wu.shape[1] // chunk
    weights(wu_hbm, wu, 0, n_chunks // 4)
    arriving.append(phase1(1))
    passing = [forward1(0)]
    for c in second:
        c.wait()

    before = (
        lax.broadcasted_iota(jnp.int32, (toks, toks), 0) < lax.broadcasted_iota(jnp.int32, (toks, toks), 1)
    ).astype(F32).astype(BF)
    n_exp = rank.shape[1]
    owners = n_exp // 2
    line = lax.broadcasted_iota(jnp.int32, (n_exp, toks), 0)
    expert = (lax.rem(line, owners) * 2 + line // owners).astype(F32)

    def ranks(n, carry):
        r = rt[n]
        named = jnp.zeros((n_exp, toks), F32)
        weight = jnp.zeros((n_exp, toks), F32)
        for k in range(chosen):
            m = (r[k : k + 1, :] == expert).astype(F32)
            named += m
            weight += m * r[8 + k : 9 + k, :]
        pos = dot(named.astype(BF), before)
        rank[n] = jnp.where(named > 0, pos, -1.0)
        wt[n] = weight
        return carry

    lax.fori_loop(0, SIDE * SIDE, ranks, 0)
    place = lax.broadcasted_iota(jnp.int32, (cap, toks), 0).astype(F32)

    def picks(j, carry):
        for h in (0, 1):
            n = x * SIDE + j if h == 0 else j * SIDE + y
            for s in (0, 1):
                for d in range(SIDE):
                    owner = y * SIDE + d if h == 0 else d * SIDE + x
                    q = rank[n, pl.ds(s * owners + owner, 1), :]
                    pick[h, j, (s * SIDE + d) * cap : (s * SIDE + d + 1) * cap, :] = (
                        (place == q).astype(F32).astype(BF)
                    )
        return carry

    lax.fori_loop(0, SIDE, picks, 0)

    passing.append(forward1(1))

    def stage(t):
        for h in (0, 1):
            mine = at.second_at(h)

            def turn(j, carry):
                got = dot(pick[h, j], p1[t, h, j]).astype(BF).reshape(2, SIDE, cap, half_w)
                st[t, h, :, :, j] = got
                return carry

            lax.fori_loop(0, SIDE, turn, 0)
            for s in (0, 1):
                own = st[t, h, s, pl.ds(mine, 1)].reshape(SIDE, cap, half_w)
                if h == 0:
                    xg[t, s, h, :, pl.ds(x, 1)] = own.reshape(SIDE, 1, cap, half_w)
                else:
                    xg[t, s, h, pl.ds(y, 1)] = own.reshape(1, SIDE, cap, half_w)

    def phase2(t, s):
        out = []
        for h in (0, 1):
            for k in steps:
                peer_at = lax.rem(at.second_at(h) + k, SIDE)
                dst = xg.at[t, s, h, :, x] if h == 0 else xg.at[t, s, h, y]
                out.append(
                    send(st.at[t, h, s, peer_at], dst, p2_s.at[t, s, h, k], p2_r.at[t, s, h, k], at.second(h, k))
                )
        return out

    moving = {}
    arrived(passing[0])
    stage(0)
    moving[0, 0] = phase2(0, 0)
    arrived(passing[1])
    stage(1)
    moving[1, 0] = phase2(1, 0)
    sent(passing[0] + passing[1])

    def slot_weights(n, carry):
        for s in (0, 1):
            q = rank[n, pl.ds(s * owners + me, 1), :]
            w = wt[n, pl.ds(s * owners + me, 1), :]
            col = jnp.sum(jnp.where(place == q, w, 0.0), axis=1, keepdims=True)
            row = (lax.rem(n, SIDE) * SIDE + n // SIDE) * cap
            wcol[s, pl.ds(pl.multiple_of(row, cap), cap), :] = jnp.broadcast_to(col, (cap, toks))
        return carry

    lax.fori_loop(0, SIDE * SIDE, slot_weights, 0)

    weights(wu_hbm, wu, n_chunks // 4, n_chunks)
    weights(wd_hbm, wd, 0, n_chunks)

    tile = 256
    h_tiles = hidden // tile
    d_tiles = 2 * half_w // tile
    per_half = half_w // tile

    def inputs(t, s, h):
        return xg[t, s, h].reshape(rows, half_w)

    def put(i, got, dst):
        cols = pl.ds(pl.multiple_of(lax.rem(i, per_half) * tile, tile), tile)
        dst[i // per_half, :, :, :, cols] = got.astype(BF).reshape(SIDE, SIDE, cap, tile)

    def forward(s):
        def turn(n, carry):
            cols = pl.ds(pl.multiple_of(n * tile, tile), tile)
            pre = dot(inputs(0, s, 0), wu[s, 0:half_w, cols]) + dot(inputs(0, s, 1), wu[s, half_w : 2 * half_w, cols])
            w = wcol[s, :, 0:1]
            sig = 1.0 / (1.0 + jnp.exp(-pre))
            right[1, s, :, cols] = (pre * sig * w).astype(BF)
            slope[s, :, cols] = sig * (1.0 + pre * (1.0 - sig)) * w
            return carry

        lax.fori_loop(0, h_tiles, turn, 0)
        sent(moving[0, s])

        def result(i, carry):
            put(i, dot(right[1, s], wd[s, pl.ds(pl.multiple_of(i * tile, tile), tile), :], 1, 1), st.at[0, :, s])
            return carry

        lax.fori_loop(0, d_tiles, result, 0)

    def core_copy(s, n):
        return pltpu.make_async_remote_copy(
            src_ref=xs.at[n % 2], dst_ref=cr.at[n], send_sem=c_s.at[s, n], recv_sem=c_r.at[s, n],
            device_id=at.other_core(), device_id_type=MESH,
        )

    def release_rows(t, s):
        for k in steps:
            for peer in (at.along_x(k), at.along_y(k)):
                pl.semaphore_signal(row_free.at[t, s], inc=1, device_id=peer, device_id_type=MESH)

    def gradient_tile(s, i, dst):
        cols = pl.ds(pl.multiple_of(lax.rem(i, per_half) * tile, tile), tile)

        def turn(t, carry):
            left = xg[t, s, i // per_half, :, :, :, cols].reshape(rows, tile)
            got = dot(left, right[t, s], 0, 0) * scale
            dst[:, pl.ds(pl.multiple_of(t * hidden, 128), hidden)] = got.astype(BF)
            return carry

        lax.fori_loop(0, 2, turn, 0)

    quarters = (2, 1, 3, 0)
    z_moving = {0: [], 1: []}

    def pair_sum(s, n):
        core_copy(s, n).wait_recv()
        step = quarters[n]
        zz = lax.rem(at.z + step, SIDE)
        own[s, zz] = (own[s, zz].astype(F32) + cr[n].astype(F32)).astype(BF)
        if step:
            z_moving[s].append(
                send(own.at[s, zz], zr.at[s, step - 1], z_s.at[s, step], z_r.at[s, step], at.along_z(step))
            )

    def backward(s):
        def turn(n, carry):
            cols = pl.ds(pl.multiple_of(n * tile, tile), tile)
            ga = dot(inputs(1, s, 0), wd[s, 0:half_w, cols]) + dot(inputs(1, s, 1), wd[s, half_w : 2 * half_w, cols])
            right[0, s, :, cols] = (ga * slope[s, :, cols]).astype(BF)
            return carry

        lax.fori_loop(0, h_tiles, turn, 0)
        if s:
            pl.semaphore_wait(core_free, 1)
        for n, step in enumerate(quarters):
            zz = lax.rem(at.z + step, SIDE)
            if n >= 2:
                core_copy(s, n - 2).wait_send()
            gradient_tile(s, zz * 2 + 1 - at.core, xs.at[n % 2])
            core_copy(s, n).start()
            gradient_tile(s, zz * 2 + at.core, own.at[s, zz])
            if n:
                pair_sum(s, n - 1)
        release_rows(1, s)

        def grad(i, carry):
            put(i, dot(right[0, s], wu[s, pl.ds(pl.multiple_of(i * tile, tile), tile), :], 1, 1), xg.at[1, s])
            return carry

        lax.fori_loop(0, d_tiles, grad, 0)
        pair_sum(s, 3)
        if s == 0:
            pl.semaphore_signal(core_free, inc=1, device_id=at.other_core(), device_id_type=MESH)
        for n in (2, 3):
            core_copy(s, n).wait_send()

    def result_rows(t, s, h, other):
        block = st.at[0, h, s] if t == 0 else xg.at[1, s, h]
        return block.at[:, other] if h == 0 else block.at[other]

    def home(t, s, h):
        return st.at[1, h, s] if t == 0 else xg.at[0, s, h]

    def return1(t, s):
        pl.semaphore_wait(row_free.at[t, s], 6)
        copies = []
        for h in (0, 1):
            mine = at.second_at(h)
            dst = home(t, s, h).at[mine]
            kept = pltpu.make_async_copy(result_rows(t, s, h, mine), dst, own_sem.at[t, s, h])
            kept.start()
            for k in steps:
                peer_at = lax.rem(mine + k, SIDE)
                copies.append(
                    send(result_rows(t, s, h, peer_at), dst, r1_s.at[t, s, h, k], r1_r.at[t, s, h, k], at.second(h, k))
                )
            copies.append(kept)
        return copies

    returning = {}
    arrived(moving[0, 0])
    moving[0, 1] = phase2(0, 1)
    forward(0)
    arrived(moving[1, 0])
    moving[1, 1] = phase2(1, 1)
    sent(moving[1, 0])
    release_rows(0, 0)
    backward(0)
    returning[0, 0] = return1(0, 0)
    returning[1, 0] = return1(1, 0)
    arrived(moving[0, 1])
    forward(1)
    arrived(moving[1, 1])
    sent(moving[1, 1])
    release_rows(0, 1)
    returning[0, 1] = return1(0, 1)
    backward(1)
    returning[1, 1] = return1(1, 1)

    last = {0: [], 1: []}

    def return2(t, h):
        for k in (2, 1, 3, 0):
            j = lax.rem(at.first_at(h) + k, SIDE)
            came = [home(t, s, h)[:, j].reshape(SIDE * cap, half_w) for s in (0, 1)]
            got = dot(pick[h, j], jnp.concatenate(came, axis=0), 0, 0)
            p1[t, h, k] = got.astype(BF)
            if k:
                last[t].append(
                    send(p1.at[t, h, k], part.at[t, h, k - 1], r2_s.at[t, h, k], r2_r.at[t, h, k], at.first(h, k))
                )

    def finish(t):
        result = (out, ig)[t]
        for c in last[t]:
            c.wait_recv()
        for h in (0, 1):
            total = p1[t, h, 0].astype(F32)
            for k in steps:
                total = total + part[t, h, k - 1].astype(F32)
            result[:, h * half_w : (h + 1) * half_w] = total.astype(BF)

    def gradients(s, keep):
        room = (ld.at[0], ld.at[1], xs.at[0])
        copies = []
        for k in (1, 3, 2):
            z_moving[s][(2, 1, 3).index(k)].wait_recv()
            copy = pltpu.make_async_copy(zr.at[s, k - 1], room[k - 1], ld_sem.at[k - 1])
            copy.start()
            copies.append(copy)
        for copy in copies:
            copy.wait()

        def turn(r, carry):
            some = pl.ds(pl.multiple_of(r * 16, 16), 16)
            total = own[s, at.z, some].astype(F32)
            for buf in room:
                total = total + buf[some].astype(F32)
            keep(r, total.astype(BF))
            return carry

        lax.fori_loop(0, xs.shape[1] // 16, turn, 0)

    def exchange(number, src_of, dst_of, along):
        copies = []
        for u in (0, 1):
            use_x = along[u]
            mine = x if use_x else y
            kept = pltpu.make_async_copy(src_of(u, mine), dst_of(u, mine), mo_sem.at[number, u])
            kept.start()
            copies.append(kept)
            for k in steps:
                peer = at.along_x(k) if use_x else at.along_y(k)
                copies.append(
                    send(
                        src_of(u, lax.rem(mine + k, SIDE)), dst_of(u, mine),
                        m_s.at[number, u, k], m_r.at[number, u, k], peer,
                    )
                )
        return copies

    relocating = []

    def spread1():
        relocating.append(
            exchange(
                0, lambda u, o: fin.at[u, :, o] if u == 0 else fin.at[u, o], lambda u, m: ra.at[u, m], (True, False)
            )
        )

    def spread2():
        relocating.append(
            exchange(
                1,
                lambda u, o: ra.at[u, :, o],
                lambda u, m: rb.at[u, m] if u == 0 else rb.at[u, :, m],
                (False, True),
            )
        )

    def gather1():
        for i in range(SIDE * SIDE):
            for u in (0, 1):
                rd[u, i // SIDE, i % SIDE] = rb[u, partner[i] // SIDE, lax.rem(partner[i], SIDE)]
        relocating.append(
            exchange(
                2, lambda u, o: rd.at[u, o] if u == 0 else rd.at[u, :, o], lambda u, m: re.at[u, m], (False, True)
            )
        )

    def gather2():
        relocating.append(
            exchange(
                3,
                lambda u, o: re.at[u, :, o],
                lambda u, m: moved_up.at[:, m] if u == 0 else moved_down.at[m],
                (True, False),
            )
        )

    def keep_first(r, total):
        for u in (0, 1):
            fin[u, r // SIDE, lax.rem(r, SIDE)] = total[:, u * hidden : (u + 1) * hidden]

    def keep_second(r, total):
        xs[1, pl.ds(pl.multiple_of(r * 16, 16), 16)] = total

    gradients(0, keep_first)
    spread1()
    arrived(relocating[0])
    spread2()
    arrived(returning[0, 0])
    arrived(returning[0, 1])
    return2(0, 0)
    return2(0, 1)
    arrived(relocating[1])
    gather1()
    arrived(returning[1, 0])
    arrived(returning[1, 1])
    return2(1, 0)
    arrived(relocating[2])
    gather2()
    return2(1, 1)
    finish(0)
    gradients(1, keep_second)
    written = []
    for u, dst in enumerate((kept_up, kept_down)):
        copy = pltpu.make_async_copy(xs.at[1, :, pl.ds(u * hidden, hidden)], dst, g_sem.at[u])
        copy.start()
        written.append(copy)
    finish(1)
    arrived(relocating[3])
    for c in written:
        c.wait()
    sent(arriving[0] + arriving[1])
    for copies in list(returning.values()) + list(last.values()) + list(z_moving.values()) + relocating:
        sent(copies)


def body(tokens, expert_ids, combine_weight, partner, w_up, w_down, out_grad):
    toks, chosen = expert_ids.shape
    width = tokens.shape[1]
    half_w = width // 2
    hidden = w_up.shape[2]
    owners = SIDE * SIDE
    cap = toks * chosen * 4 // (3 * 2 * owners)
    rows = owners * cap
    any_ = pl.BlockSpec(memory_space=pl.ANY)
    vmem = pl.BlockSpec(memory_space=pltpu.VMEM)
    n_rows = width // (2 * SIDE)
    piece = n_rows // owners
    tile_shape = jax.ShapeDtypeStruct((n_rows, hidden), BF)
    piece_shape = (SIDE, SIDE, piece, hidden)
    output, input_grad, moved_up, moved_down, kept_up, kept_down, *_ = pl.pallas_call(
        functools.partial(kernel, cap, chosen, 1.0 / toks),
        out_shape=(
            jax.ShapeDtypeStruct((toks, width), BF),
            jax.ShapeDtypeStruct((toks, width), BF),
            jax.ShapeDtypeStruct(piece_shape, BF),
            jax.ShapeDtypeStruct(piece_shape, BF),
            tile_shape,
            tile_shape,
            jax.ShapeDtypeStruct((2, SIDE - 1, n_rows, 2 * hidden), BF),
            jax.ShapeDtypeStruct((2, *piece_shape), BF),
            jax.ShapeDtypeStruct((2, *piece_shape), BF),
        ),
        in_specs=[pl.BlockSpec(memory_space=pltpu.SMEM), vmem, vmem, any_, any_, any_, any_],
        out_specs=(vmem, vmem, any_, any_, any_, any_, any_, any_, any_),
        scratch_shapes=[
            pltpu.VMEM((owners, 16, toks), F32),
            pltpu.VMEM((owners, 2 * owners, toks), F32),
            pltpu.VMEM((owners, 2 * owners, toks), F32),
            pltpu.VMEM((2, SIDE, 2 * SIDE * cap, toks), BF),
            pltpu.VMEM((2, 2, SIDE, toks, half_w), BF),
            pltpu.VMEM((2, 2, 2, SIDE, SIDE, cap, half_w), BF),
            pltpu.VMEM((2, 2, 2, SIDE, SIDE, cap, half_w), BF),
            pltpu.VMEM((2, width, hidden), BF),
            pltpu.VMEM((2, width, hidden), BF),
            pltpu.VMEM((2, 128, 2, hidden), BF),
            pltpu.VMEM((2, rows, toks), F32),
            pltpu.VMEM((2, rows, hidden), F32),
            pltpu.VMEM((2, 2, rows, hidden), BF),
            pltpu.VMEM((2, 2, SIDE - 1, toks, half_w), BF),
            pltpu.VMEM((2, SIDE, n_rows, 2 * hidden), BF),
            pltpu.VMEM((2, n_rows, 2 * hidden), BF),
            pltpu.VMEM((2, n_rows, 2 * hidden), BF),
            pltpu.VMEM((SIDE, n_rows, 2 * hidden), BF),
            pltpu.VMEM((2, *piece_shape), BF),
            pltpu.VMEM((2, *piece_shape), BF),
            pltpu.VMEM((2, *piece_shape), BF),
            DMA((2, 4)), DMA((2, 4)),
            DMA((2, 2, 4)), DMA((2, 2, 4)), DMA((2, 2)),
            DMA((2, 2, 2, 4)), DMA((2, 2, 2, 4)),
            DMA((2,)),
            DMA((2, 2, 2, 4)), DMA((2, 2, 2, 4)), DMA((2, 2, 2)),
            DMA((2, 2, 4)), DMA((2, 2, 4)),
            DMA((2, 4)), DMA((2, 4)), DMA((2, 4)), DMA((2, 4)), DMA((3,)), DMA((2,)),
            DMA((4, 2, 4)), DMA((4, 2, 4)), DMA((4, 2)),
            pltpu.SemaphoreType.REGULAR((2, 2)), pltpu.SemaphoreType.REGULAR,
        ],
        compiler_params=pltpu.CompilerParams(
            collective_id=0, has_side_effects=True, vmem_limit_bytes=62 << 20
        ),
    )(partner, expert_ids.T, combine_weight.T, tokens, out_grad, w_up, w_down)

    grad_up = jnp.stack([moved_up.reshape(n_rows, hidden), kept_up], axis=1)
    grad_down = jnp.stack([moved_down.reshape(n_rows, hidden), kept_down], axis=1)
    return (output, input_grad, grad_up, grad_down)


def solution(mesh):
    return jax.shard_map(
        body,
        mesh=mesh,
        in_specs=(
            P(("dp", "expert"), None),
            P(("dp", "expert"), None),
            P(("dp", "expert"), None),
            P(),
            P(None, "expert", None),
            P(None, "expert", None),
            P(("dp", "expert"), None),
        ),
        out_specs=(
            P(("dp", "expert"), None),
            P(("dp", "expert"), None),
            P("dp", "expert", None),
            P("dp", "expert", None),
        ),
        check_vma=False,
    )
```

```python
import functools

import jax
import jax.numpy as jnp
from jax import lax
from jax.experimental import pallas as pl
from jax.experimental.pallas import tpu as pltpu
from jax.sharding import PartitionSpec as P

MESH = pl.DeviceIdType.MESH
BF = jnp.bfloat16
F32 = jnp.float32
DMA = pltpu.SemaphoreType.DMA
SIDE = 4


class Place:
    def __init__(self):
        self.dp = lax.axis_index("dp")
        self.me = lax.axis_index("expert")
        self.y = self.me // SIDE
        self.x = lax.rem(self.me, SIDE)
        self.z = self.dp // 2
        self.core = lax.rem(self.dp, 2)

    def along_y(self, step):
        return (self.dp, lax.rem(self.y + step, SIDE) * SIDE + self.x)

    def along_x(self, step):
        return (self.dp, self.y * SIDE + lax.rem(self.x + step, SIDE))

    def first(self, half, step):
        return self.along_y(step) if half == 0 else self.along_x(step)

    def second(self, half, step):
        return self.along_x(step) if half == 0 else self.along_y(step)

    def first_at(self, half):
        return self.y if half == 0 else self.x

    def second_at(self, half):
        return self.x if half == 0 else self.y

    def along_z(self, step):
        return (lax.rem(self.z + step, SIDE) * 2 + self.core, self.me)

    def other_core(self):
        return (self.z * 2 + 1 - self.core, self.me)

    def greet(self):
        barrier = pltpu.get_barrier_semaphore()
        peers = [self.other_core()]
        for step in (1, 2, 3):
            peers += [self.along_y(step), self.along_x(step), self.along_z(step)]
        for peer in peers:
            pl.semaphore_signal(barrier, inc=1, device_id=peer, device_id_type=MESH)
        pl.semaphore_wait(barrier, len(peers))


def send(src, dst, send_sem, recv_sem, peer):
    copy = pltpu.make_async_remote_copy(
        src_ref=src, dst_ref=dst, send_sem=send_sem, recv_sem=recv_sem, device_id=peer, device_id_type=MESH
    )
    copy.start()
    return copy


def dot(a, b, over_a=1, over_b=0):
    return lax.dot_general(a, b, (((over_a,), (over_b,)), ((), ())), preferred_element_type=F32)


def kernel(
    cap, chosen, scale,
    partner, ids, gate, tok, og, wu_hbm, wd_hbm,
    out, ig, moved_up, moved_down, kept_up, kept_down, zr, ra, re,
    rt, rank, wt, pick, p1, st, xg, wu, wd, wbuf, wcol, slope, right, part, own, xs, ld, cr, fin, rb, rd,
    rt_s, rt_r, p1_s, p1_r, p1_o, p2_s, p2_r, w_sem, r1_s, r1_r, own_sem, r2_s, r2_r,
    c_s, c_r, z_s, z_r, ld_sem, g_sem, m_s, m_r, mo_sem, row_free, core_free,
):
    at = Place()
    x, y, me = at.x, at.y, at.me
    toks = tok.shape[0]
    half_w = tok.shape[1] // 2
    hidden = wu.shape[2]
    rows = SIDE * SIDE * cap
    chunk = wbuf.shape[1]
    steps = (1, 2, 3)

    at.greet()
    route = rt.at[x * SIDE + y]
    route[0:chosen] = ids[...].astype(F32)
    route[8 : 8 + chosen] = gate[...]
    first = [send(route, route, rt_s.at[0, k], rt_r.at[0, k], at.along_y(k)) for k in steps]

    def arrived(copies):
        for c in copies:
            if c.is_remote:
                c.wait_recv()
            else:
                c.wait()

    def sent(copies):
        for c in copies:
            if c.is_remote:
                c.wait_send()

    def phase1(t):
        copies = []
        for h in (0, 1):
            block = (tok, og)[t].at[:, pl.ds(h * half_w, half_w)]
            dst = p1.at[t, h, at.first_at(h)]
            for k in (1, 3):
                copies.append(send(block, dst, p1_s.at[t, h, k], p1_r.at[t, h, k], at.first(h, k)))
            kept = pltpu.make_async_copy(block, dst, p1_o.at[t, h])
            kept.start()
            copies.append(kept)
        return copies

    def forward1(t):
        copies = []
        part_rows = toks // 2
        for h in (0, 1):
            for k, sem in ((1, 2), (3, 0)):
                arriving[t][3 * h + k // 2].wait_recv()
                origin = lax.rem(at.first_at(h) + SIDE - k, SIDE)
                block = p1.at[t, h, origin, pl.ds((k // 2) * part_rows, part_rows)]
                copies.append(send(block, block, p1_s.at[t, h, sem], p1_r.at[t, h, sem], at.first(h, k)))
            arriving[t][3 * h + 2].wait()
        return copies

    def weights(hbm, vmem, lo, hi):
        def fetch(i):
            slot = lax.rem(i, 2)
            return pltpu.make_async_copy(
                hbm.at[pl.ds(pl.multiple_of(i * chunk, chunk), chunk)], wbuf.at[slot], w_sem.at[slot]
            )

        fetch(lo).start()

        def turn(i, carry):
            @pl.when(i + 1 < hi)
            def _():
                fetch(i + 1).start()

            fetch(i).wait()
            vmem[:, pl.ds(pl.multiple_of(i * chunk, chunk), chunk), :] = jnp.swapaxes(
                wbuf[lax.rem(i, 2)], 0, 1
            )
            return carry

        lax.fori_loop(lo, hi, turn, 0)

    for c in first:
        c.wait()
    block = rt.at[pl.ds(x * SIDE, SIDE)]
    second = [send(block, block, rt_s.at[1, k], rt_r.at[1, k], at.along_x(k)) for k in steps]
    arriving = [phase1(0)]
    n_chunks = wu.shape[1] // chunk
    weights(wu_hbm, wu, 0, n_chunks // 4)
    arriving.append(phase1(1))
    passing = [forward1(0)]
    for c in second:
        c.wait()

    before = (
        lax.broadcasted_iota(jnp.int32, (toks, toks), 0) < lax.broadcasted_iota(jnp.int32, (toks, toks), 1)
    ).astype(F32).astype(BF)
    n_exp = rank.shape[1]
    owners = n_exp // 2
    line = lax.broadcasted_iota(jnp.int32, (n_exp, toks), 0)
    expert = (lax.rem(line, owners) * 2 + line // owners).astype(F32)

    def ranks(n, carry):
        r = rt[n]
        named = jnp.zeros((n_exp, toks), F32)
        weight = jnp.zeros((n_exp, toks), F32)
        for k in range(chosen):
            m = (r[k : k + 1, :] == expert).astype(F32)
            named += m
            weight += m * r[8 + k : 9 + k, :]
        pos = dot(named.astype(BF), before)
        rank[n] = jnp.where(named > 0, pos, -1.0)
        wt[n] = weight
        return carry

    lax.fori_loop(0, SIDE * SIDE, ranks, 0)
    place = lax.broadcasted_iota(jnp.int32, (cap, toks), 0).astype(F32)

    def picks(j, carry):
        for h in (0, 1):
            n = x * SIDE + j if h == 0 else j * SIDE + y
            for s in (0, 1):
                for d in range(SIDE):
                    owner = y * SIDE + d if h == 0 else d * SIDE + x
                    q = rank[n, pl.ds(s * owners + owner, 1), :]
                    pick[h, j, (s * SIDE + d) * cap : (s * SIDE + d + 1) * cap, :] = (
                        (place == q).astype(F32).astype(BF)
                    )
        return carry

    lax.fori_loop(0, SIDE, picks, 0)

    passing.append(forward1(1))

    def stage(t):
        for h in (0, 1):
            mine = at.second_at(h)

            def turn(j, carry):
                got = dot(pick[h, j], p1[t, h, j]).astype(BF).reshape(2, SIDE, cap, half_w)
                st[t, h, :, :, j] = got
                return carry

            lax.fori_loop(0, SIDE, turn, 0)
            for s in (0, 1):
                own = st[t, h, s, pl.ds(mine, 1)].reshape(SIDE, cap, half_w)
                if h == 0:
                    xg[t, s, h, :, pl.ds(x, 1)] = own.reshape(SIDE, 1, cap, half_w)
                else:
                    xg[t, s, h, pl.ds(y, 1)] = own.reshape(1, SIDE, cap, half_w)

    def phase2(t, s):
        out = []
        for h in (0, 1):
            for k in steps:
                peer_at = lax.rem(at.second_at(h) + k, SIDE)
                dst = xg.at[t, s, h, :, x] if h == 0 else xg.at[t, s, h, y]
                out.append(
                    send(st.at[t, h, s, peer_at], dst, p2_s.at[t, s, h, k], p2_r.at[t, s, h, k], at.second(h, k))
                )
        return out

    moving = {}
    arrived(passing[0])
    stage(0)
    moving[0, 0] = phase2(0, 0)
    arrived(passing[1])
    stage(1)
    moving[1, 0] = phase2(1, 0)
    sent(passing[0] + passing[1])

    def slot_weights(n, carry):
        for s in (0, 1):
            q = rank[n, pl.ds(s * owners + me, 1), :]
            w = wt[n, pl.ds(s * owners + me, 1), :]
            col = jnp.sum(jnp.where(place == q, w, 0.0), axis=1, keepdims=True)
            row = (lax.rem(n, SIDE) * SIDE + n // SIDE) * cap
            wcol[s, pl.ds(pl.multiple_of(row, cap), cap), :] = jnp.broadcast_to(col, (cap, toks))
        return carry

    lax.fori_loop(0, SIDE * SIDE, slot_weights, 0)

    weights(wu_hbm, wu, n_chunks // 4, n_chunks)
    weights(wd_hbm, wd, 0, n_chunks)

    tile = 256
    h_tiles = hidden // tile
    d_tiles = 2 * half_w // tile
    per_half = half_w // tile

    def inputs(t, s, h):
        return xg[t, s, h].reshape(rows, half_w)

    def put(i, got, dst):
        cols = pl.ds(pl.multiple_of(lax.rem(i, per_half) * tile, tile), tile)
        dst[i // per_half, :, :, :, cols] = got.astype(BF).reshape(SIDE, SIDE, cap, tile)

    def forward(s):
        def turn(n, carry):
            cols = pl.ds(pl.multiple_of(n * tile, tile), tile)
            pre = dot(inputs(0, s, 0), wu[s, 0:half_w, cols]) + dot(inputs(0, s, 1), wu[s, half_w : 2 * half_w, cols])
            w = wcol[s, :, 0:1]
            sig = 1.0 / (1.0 + jnp.exp(-pre))
            right[1, s, :, cols] = (pre * sig * w).astype(BF)
            slope[s, :, cols] = sig * (1.0 + pre * (1.0 - sig)) * w
            return carry

        lax.fori_loop(0, h_tiles, turn, 0)
        sent(moving[0, s])

        def result(i, carry):
            put(i, dot(right[1, s], wd[s, pl.ds(pl.multiple_of(i * tile, tile), tile), :], 1, 1), st.at[0, :, s])
            return carry

        lax.fori_loop(0, d_tiles, result, 0)

    def core_copy(s, n):
        return pltpu.make_async_remote_copy(
            src_ref=xs.at[n % 2], dst_ref=cr.at[n], send_sem=c_s.at[s, n], recv_sem=c_r.at[s, n],
            device_id=at.other_core(), device_id_type=MESH,
        )

    def release_rows(t, s):
        for k in steps:
            for peer in (at.along_x(k), at.along_y(k)):
                pl.semaphore_signal(row_free.at[t, s], inc=1, device_id=peer, device_id_type=MESH)

    def gradient_tile(s, i, dst):
        cols = pl.ds(pl.multiple_of(lax.rem(i, per_half) * tile, tile), tile)

        def turn(t, carry):
            left = xg[t, s, i // per_half, :, :, :, cols].reshape(rows, tile)
            got = dot(left, right[t, s], 0, 0) * scale
            dst[:, pl.ds(pl.multiple_of(t * hidden, 128), hidden)] = got.astype(BF)
            return carry

        lax.fori_loop(0, 2, turn, 0)

    quarters = (2, 1, 3, 0)
    z_moving = {0: [], 1: []}

    def pair_sum(s, n):
        core_copy(s, n).wait_recv()
        step = quarters[n]
        zz = lax.rem(at.z + step, SIDE)
        own[s, zz] = (own[s, zz].astype(F32) + cr[n].astype(F32)).astype(BF)
        if step:
            z_moving[s].append(
                send(own.at[s, zz], zr.at[s, step - 1], z_s.at[s, step], z_r.at[s, step], at.along_z(step))
            )

    def backward(s):
        def turn(n, carry):
            cols = pl.ds(pl.multiple_of(n * tile, tile), tile)
            ga = dot(inputs(1, s, 0), wd[s, 0:half_w, cols]) + dot(inputs(1, s, 1), wd[s, half_w : 2 * half_w, cols])
            right[0, s, :, cols] = (ga * slope[s, :, cols]).astype(BF)
            return carry

        lax.fori_loop(0, h_tiles, turn, 0)
        if s:
            pl.semaphore_wait(core_free, 1)
        for n, step in enumerate(quarters):
            zz = lax.rem(at.z + step, SIDE)
            if n >= 2:
                core_copy(s, n - 2).wait_send()
            gradient_tile(s, zz * 2 + 1 - at.core, xs.at[n % 2])
            core_copy(s, n).start()
            gradient_tile(s, zz * 2 + at.core, own.at[s, zz])
            if n:
                pair_sum(s, n - 1)
        release_rows(1, s)

        def grad(i, carry):
            put(i, dot(right[0, s], wu[s, pl.ds(pl.multiple_of(i * tile, tile), tile), :], 1, 1), xg.at[1, s])
            return carry

        lax.fori_loop(0, d_tiles, grad, 0)
        pair_sum(s, 3)
        if s == 0:
            pl.semaphore_signal(core_free, inc=1, device_id=at.other_core(), device_id_type=MESH)
        for n in (2, 3):
            core_copy(s, n).wait_send()

    def result_rows(t, s, h, other):
        block = st.at[0, h, s] if t == 0 else xg.at[1, s, h]
        return block.at[:, other] if h == 0 else block.at[other]

    def home(t, s, h):
        return st.at[1, h, s] if t == 0 else xg.at[0, s, h]

    def return1(t, s):
        pl.semaphore_wait(row_free.at[t, s], 6)
        copies = []
        for h in (0, 1):
            mine = at.second_at(h)
            dst = home(t, s, h).at[mine]
            kept = pltpu.make_async_copy(result_rows(t, s, h, mine), dst, own_sem.at[t, s, h])
            kept.start()
            for k in steps:
                peer_at = lax.rem(mine + k, SIDE)
                copies.append(
                    send(result_rows(t, s, h, peer_at), dst, r1_s.at[t, s, h, k], r1_r.at[t, s, h, k], at.second(h, k))
                )
            copies.append(kept)
        return copies

    returning = {}
    arrived(moving[0, 0])
    moving[0, 1] = phase2(0, 1)
    forward(0)
    arrived(moving[1, 0])
    moving[1, 1] = phase2(1, 1)
    sent(moving[1, 0])
    release_rows(0, 0)
    backward(0)
    returning[0, 0] = return1(0, 0)
    returning[1, 0] = return1(1, 0)
    arrived(moving[0, 1])
    forward(1)
    arrived(moving[1, 1])
    sent(moving[1, 1])
    release_rows(0, 1)
    returning[0, 1] = return1(0, 1)
    backward(1)
    returning[1, 1] = return1(1, 1)

    last = {0: [], 1: []}
    homing = {0: [], 1: []}

    def return2(t):
        for h in (0, 1):
            for k in (2, 1, 3, 0):
                j = lax.rem(at.first_at(h) + k, SIDE)
                came = [home(t, s, h)[:, j].reshape(SIDE * cap, half_w) for s in (0, 1)]
                p1[t, h, k] = dot(pick[h, j], jnp.concatenate(came, axis=0), 0, 0).astype(BF)
                if k == 2:
                    for way, sem in ((1, 2), (3, 0)):
                        some = pl.ds((way // 2) * (toks // 2), toks // 2)
                        last[t].append(
                            send(
                                p1.at[t, h, 2, some], part.at[t, h, 1, some],
                                r2_s.at[t, h, sem], r2_r.at[t, h, sem], at.first(h, way),
                            )
                        )

    def return3(t):
        for c in last[t]:
            c.wait_recv()
        for h in (0, 1):
            for k in (1, 3):
                some = slice((k // 2) * (toks // 2), (k // 2 + 1) * (toks // 2))
                total = p1[t, h, k, some].astype(F32) + part[t, h, 1, some].astype(F32)
                p1[t, h, k, some] = total.astype(BF)
                homing[t].append(
                    send(p1.at[t, h, k], part.at[t, h, k - 1], r2_s.at[t, h, k], r2_r.at[t, h, k], at.first(h, k))
                )

    def finish(t):
        result = (out, ig)[t]
        for c in homing[t]:
            c.wait_recv()
        for h in (0, 1):
            total = p1[t, h, 0].astype(F32)
            for k in (1, 3):
                total = total + part[t, h, k - 1].astype(F32)
            result[:, h * half_w : (h + 1) * half_w] = total.astype(BF)

    def gradients(s, keep):
        room = (ld.at[0], ld.at[1], xs.at[0])
        copies = []
        for k in (1, 3, 2):
            z_moving[s][(2, 1, 3).index(k)].wait_recv()
            copy = pltpu.make_async_copy(zr.at[s, k - 1], room[k - 1], ld_sem.at[k - 1])
            copy.start()
            copies.append(copy)
        for copy in copies:
            copy.wait()

        def turn(r, carry):
            some = pl.ds(pl.multiple_of(r * 16, 16), 16)
            total = own[s, at.z, some].astype(F32)
            for buf in room:
                total = total + buf[some].astype(F32)
            keep(r, total.astype(BF))
            return carry

        lax.fori_loop(0, xs.shape[1] // 16, turn, 0)

    def exchange(number, src_of, dst_of, along):
        copies = []
        for u in (0, 1):
            use_x = along[u]
            mine = x if use_x else y
            kept = pltpu.make_async_copy(src_of(u, mine), dst_of(u, mine), mo_sem.at[number, u])
            kept.start()
            copies.append(kept)
            for k in steps:
                peer = at.along_x(k) if use_x else at.along_y(k)
                copies.append(
                    send(
                        src_of(u, lax.rem(mine + k, SIDE)), dst_of(u, mine),
                        m_s.at[number, u, k], m_r.at[number, u, k], peer,
                    )
                )
        return copies

    relocating = []

    def spread1():
        relocating.append(
            exchange(
                0, lambda u, o: fin.at[u, :, o] if u == 0 else fin.at[u, o], lambda u, m: ra.at[u, m], (True, False)
            )
        )

    def spread2():
        relocating.append(
            exchange(
                1,
                lambda u, o: ra.at[u, :, o],
                lambda u, m: rb.at[u, m] if u == 0 else rb.at[u, :, m],
                (False, True),
            )
        )

    def gather1():
        for i in range(SIDE * SIDE):
            for u in (0, 1):
                rd[u, i // SIDE, i % SIDE] = rb[u, partner[i] // SIDE, lax.rem(partner[i], SIDE)]
        relocating.append(
            exchange(
                2, lambda u, o: rd.at[u, o] if u == 0 else rd.at[u, :, o], lambda u, m: re.at[u, m], (False, True)
            )
        )

    def gather2():
        relocating.append(
            exchange(
                3,
                lambda u, o: re.at[u, :, o],
                lambda u, m: moved_up.at[:, m] if u == 0 else moved_down.at[m],
                (True, False),
            )
        )

    def keep_first(r, total):
        for u in (0, 1):
            fin[u, r // SIDE, lax.rem(r, SIDE)] = total[:, u * hidden : (u + 1) * hidden]

    def keep_second(r, total):
        xs[1, pl.ds(pl.multiple_of(r * 16, 16), 16)] = total

    gradients(0, keep_first)
    spread1()
    arrived(relocating[0])
    spread2()
    arrived(returning[0, 0])
    arrived(returning[0, 1])
    return2(0)
    arrived(relocating[1])
    gather1()
    return3(0)
    arrived(returning[1, 0])
    arrived(returning[1, 1])
    return2(1)
    arrived(relocating[2])
    gather2()
    return3(1)
    finish(0)
    gradients(1, keep_second)
    written = []
    for u, dst in enumerate((kept_up, kept_down)):
        copy = pltpu.make_async_copy(xs.at[1, :, pl.ds(u * hidden, hidden)], dst, g_sem.at[u])
        copy.start()
        written.append(copy)
    finish(1)
    arrived(relocating[3])
    for c in written:
        c.wait()
    sent(arriving[0] + arriving[1])
    for copies in list(returning.values()) + list(last.values()) + list(homing.values()) + list(z_moving.values()) + relocating:
        sent(copies)


def body(tokens, expert_ids, combine_weight, partner, w_up, w_down, out_grad):
    toks, chosen = expert_ids.shape
    width = tokens.shape[1]
    half_w = width // 2
    hidden = w_up.shape[2]
    owners = SIDE * SIDE
    cap = toks * chosen * 4 // (3 * 2 * owners)
    rows = owners * cap
    any_ = pl.BlockSpec(memory_space=pl.ANY)
    vmem = pl.BlockSpec(memory_space=pltpu.VMEM)
    n_rows = width // (2 * SIDE)
    piece = n_rows // owners
    tile_shape = jax.ShapeDtypeStruct((n_rows, hidden), BF)
    piece_shape = (SIDE, SIDE, piece, hidden)
    output, input_grad, moved_up, moved_down, kept_up, kept_down, *_ = pl.pallas_call(
        functools.partial(kernel, cap, chosen, 1.0 / toks),
        out_shape=(
            jax.ShapeDtypeStruct((toks, width), BF),
            jax.ShapeDtypeStruct((toks, width), BF),
            jax.ShapeDtypeStruct(piece_shape, BF),
            jax.ShapeDtypeStruct(piece_shape, BF),
            tile_shape,
            tile_shape,
            jax.ShapeDtypeStruct((2, SIDE - 1, n_rows, 2 * hidden), BF),
            jax.ShapeDtypeStruct((2, *piece_shape), BF),
            jax.ShapeDtypeStruct((2, *piece_shape), BF),
        ),
        in_specs=[pl.BlockSpec(memory_space=pltpu.SMEM), vmem, vmem, any_, any_, any_, any_],
        out_specs=(vmem, vmem, any_, any_, any_, any_, any_, any_, any_),
        scratch_shapes=[
            pltpu.VMEM((owners, 16, toks), F32),
            pltpu.VMEM((owners, 2 * owners, toks), F32),
            pltpu.VMEM((owners, 2 * owners, toks), F32),
            pltpu.VMEM((2, SIDE, 2 * SIDE * cap, toks), BF),
            pltpu.VMEM((2, 2, SIDE, toks, half_w), BF),
            pltpu.VMEM((2, 2, 2, SIDE, SIDE, cap, half_w), BF),
            pltpu.VMEM((2, 2, 2, SIDE, SIDE, cap, half_w), BF),
            pltpu.VMEM((2, width, hidden), BF),
            pltpu.VMEM((2, width, hidden), BF),
            pltpu.VMEM((2, 128, 2, hidden), BF),
            pltpu.VMEM((2, rows, toks), F32),
            pltpu.VMEM((2, rows, hidden), F32),
            pltpu.VMEM((2, 2, rows, hidden), BF),
            pltpu.VMEM((2, 2, SIDE - 1, toks, half_w), BF),
            pltpu.VMEM((2, SIDE, n_rows, 2 * hidden), BF),
            pltpu.VMEM((2, n_rows, 2 * hidden), BF),
            pltpu.VMEM((2, n_rows, 2 * hidden), BF),
            pltpu.VMEM((SIDE, n_rows, 2 * hidden), BF),
            pltpu.VMEM((2, *piece_shape), BF),
            pltpu.VMEM((2, *piece_shape), BF),
            pltpu.VMEM((2, *piece_shape), BF),
            DMA((2, 4)), DMA((2, 4)),
            DMA((2, 2, 4)), DMA((2, 2, 4)), DMA((2, 2)),
            DMA((2, 2, 2, 4)), DMA((2, 2, 2, 4)),
            DMA((2,)),
            DMA((2, 2, 2, 4)), DMA((2, 2, 2, 4)), DMA((2, 2, 2)),
            DMA((2, 2, 4)), DMA((2, 2, 4)),
            DMA((2, 4)), DMA((2, 4)), DMA((2, 4)), DMA((2, 4)), DMA((3,)), DMA((2,)),
            DMA((4, 2, 4)), DMA((4, 2, 4)), DMA((4, 2)),
            pltpu.SemaphoreType.REGULAR((2, 2)), pltpu.SemaphoreType.REGULAR,
        ],
        compiler_params=pltpu.CompilerParams(
            collective_id=0, has_side_effects=True, vmem_limit_bytes=62 << 20
        ),
    )(partner, expert_ids.T, combine_weight.T, tokens, out_grad, w_up, w_down)

    grad_up = jnp.stack([moved_up.reshape(n_rows, hidden), kept_up], axis=1)
    grad_down = jnp.stack([moved_down.reshape(n_rows, hidden), kept_down], axis=1)
    return (output, input_grad, grad_up, grad_down)


def solution(mesh):
    return jax.shard_map(
        body,
        mesh=mesh,
        in_specs=(
            P(("dp", "expert"), None),
            P(("dp", "expert"), None),
            P(("dp", "expert"), None),
            P(),
            P(None, "expert", None),
            P(None, "expert", None),
            P(("dp", "expert"), None),
        ),
        out_specs=(
            P(("dp", "expert"), None),
            P(("dp", "expert"), None),
            P("dp", "expert", None),
            P("dp", "expert", None),
        ),
        check_vma=False,
    )
```

```python
import functools

import jax
import jax.numpy as jnp
from jax import lax
from jax.experimental import pallas as pl
from jax.experimental.pallas import tpu as pltpu
from jax.sharding import PartitionSpec as P

MESH = pl.DeviceIdType.MESH
BF = jnp.bfloat16
F32 = jnp.float32
DMA = pltpu.SemaphoreType.DMA
SIDE = 4


class Place:
    def __init__(self):
        self.dp = lax.axis_index("dp")
        self.me = lax.axis_index("expert")
        self.y = self.me // SIDE
        self.x = lax.rem(self.me, SIDE)
        self.z = self.dp // 2
        self.core = lax.rem(self.dp, 2)

    def along_y(self, step):
        return (self.dp, lax.rem(self.y + step, SIDE) * SIDE + self.x)

    def along_x(self, step):
        return (self.dp, self.y * SIDE + lax.rem(self.x + step, SIDE))

    def first(self, half, step):
        return self.along_y(step) if half == 0 else self.along_x(step)

    def second(self, half, step):
        return self.along_x(step) if half == 0 else self.along_y(step)

    def first_at(self, half):
        return self.y if half == 0 else self.x

    def second_at(self, half):
        return self.x if half == 0 else self.y

    def along_z(self, step):
        return (lax.rem(self.z + step, SIDE) * 2 + self.core, self.me)

    def other_core(self):
        return (self.z * 2 + 1 - self.core, self.me)

    def greet(self):
        barrier = pltpu.get_barrier_semaphore()
        peers = [self.other_core()]
        for step in (1, 2, 3):
            peers += [self.along_y(step), self.along_x(step), self.along_z(step)]
        for peer in peers:
            pl.semaphore_signal(barrier, inc=1, device_id=peer, device_id_type=MESH)
        pl.semaphore_wait(barrier, len(peers))


def send(src, dst, send_sem, recv_sem, peer):
    copy = pltpu.make_async_remote_copy(
        src_ref=src, dst_ref=dst, send_sem=send_sem, recv_sem=recv_sem, device_id=peer, device_id_type=MESH
    )
    copy.start()
    return copy


def dot(a, b, over_a=1, over_b=0):
    return lax.dot_general(a, b, (((over_a,), (over_b,)), ((), ())), preferred_element_type=F32)


def kernel(
    cap, chosen, scale,
    partner, ids, gate, tok, og, wu_hbm, wd_hbm,
    out, ig, moved_up, moved_down, kept_up, kept_down, zr, ra, re,
    rt, rank, wt, pick, p1, st, xg, wu, wd, wbuf, wcol, slope, right, part, own, xs, ld, cr, fin, rb, rd,
    rt_s, rt_r, p1_s, p1_r, p1_o, p2_s, p2_r, w_sem, r1_s, r1_r, own_sem, r2_s, r2_r,
    c_s, c_r, z_s, z_r, ld_sem, g_sem, m_s, m_r, mo_sem, row_free, core_free,
):
    at = Place()
    x, y, me = at.x, at.y, at.me
    toks = tok.shape[0]
    half_w = tok.shape[1] // 2
    hidden = wu.shape[2]
    rows = SIDE * SIDE * cap
    chunk = wbuf.shape[1]
    steps = (1, 2, 3)

    at.greet()
    route = rt.at[x * SIDE + y]
    route[0:chosen] = ids[...].astype(F32)
    route[8 : 8 + chosen] = gate[...]
    first = [send(route, route, rt_s.at[0, k], rt_r.at[0, k], at.along_y(k)) for k in steps]

    def arrived(copies):
        for c in copies:
            if c.is_remote:
                c.wait_recv()
            else:
                c.wait()

    def sent(copies):
        for c in copies:
            if c.is_remote:
                c.wait_send()

    def phase1(t):
        copies = []
        for h in (0, 1):
            block = (tok, og)[t].at[:, pl.ds(h * half_w, half_w)]
            dst = p1.at[t, h, at.first_at(h)]
            for k in (1, 3):
                copies.append(send(block, dst, p1_s.at[t, h, k], p1_r.at[t, h, k], at.first(h, k)))
            kept = pltpu.make_async_copy(block, dst, p1_o.at[t, h])
            kept.start()
            copies.append(kept)
        return copies

    def forward1(t):
        copies = []
        part_rows = toks // 2
        for h in (0, 1):
            for k, sem in ((1, 2), (3, 0)):
                arriving[t][3 * h + k // 2].wait_recv()
                origin = lax.rem(at.first_at(h) + SIDE - k, SIDE)
                block = p1.at[t, h, origin, pl.ds((k // 2) * part_rows, part_rows)]
                copies.append(send(block, block, p1_s.at[t, h, sem], p1_r.at[t, h, sem], at.first(h, k)))
            arriving[t][3 * h + 2].wait()
        return copies

    def weights(hbm, vmem, lo, hi):
        def fetch(i):
            slot = lax.rem(i, 2)
            return pltpu.make_async_copy(
                hbm.at[pl.ds(pl.multiple_of(i * chunk, chunk), chunk)], wbuf.at[slot], w_sem.at[slot]
            )

        fetch(lo).start()

        def turn(i, carry):
            @pl.when(i + 1 < hi)
            def _():
                fetch(i + 1).start()

            fetch(i).wait()
            vmem[:, pl.ds(pl.multiple_of(i * chunk, chunk), chunk), :] = jnp.swapaxes(
                wbuf[lax.rem(i, 2)], 0, 1
            )
            return carry

        lax.fori_loop(lo, hi, turn, 0)

    arriving = [phase1(0)]
    for c in first:
        c.wait()
    block = rt.at[pl.ds(x * SIDE, SIDE)]
    second = [send(block, block, rt_s.at[1, k], rt_r.at[1, k], at.along_x(k)) for k in steps]
    n_chunks = wu.shape[1] // chunk
    weights(wu_hbm, wu, 0, n_chunks // 4)
    arriving.append(phase1(1))
    passing = [forward1(0)]
    for c in second:
        c.wait()

    before = (
        lax.broadcasted_iota(jnp.int32, (toks, toks), 0) < lax.broadcasted_iota(jnp.int32, (toks, toks), 1)
    ).astype(F32).astype(BF)
    n_exp = rank.shape[1]
    owners = n_exp // 2
    line = lax.broadcasted_iota(jnp.int32, (n_exp, toks), 0)
    expert = (lax.rem(line, owners) * 2 + line // owners).astype(F32)

    def ranks(n, carry):
        r = rt[n]
        named = jnp.zeros((n_exp, toks), F32)
        weight = jnp.zeros((n_exp, toks), F32)
        for k in range(chosen):
            m = (r[k : k + 1, :] == expert).astype(F32)
            named += m
            weight += m * r[8 + k : 9 + k, :]
        pos = dot(named.astype(BF), before)
        rank[n] = jnp.where(named > 0, pos, -1.0)
        wt[n] = weight
        return carry

    lax.fori_loop(0, SIDE * SIDE, ranks, 0)
    place = lax.broadcasted_iota(jnp.int32, (cap, toks), 0).astype(F32)

    def picks(j, carry):
        for h in (0, 1):
            n = x * SIDE + j if h == 0 else j * SIDE + y
            for s in (0, 1):
                for d in range(SIDE):
                    owner = y * SIDE + d if h == 0 else d * SIDE + x
                    q = rank[n, pl.ds(s * owners + owner, 1), :]
                    pick[h, j, (s * SIDE + d) * cap : (s * SIDE + d + 1) * cap, :] = (
                        (place == q).astype(F32).astype(BF)
                    )
        return carry

    lax.fori_loop(0, SIDE, picks, 0)

    passing.append(forward1(1))

    def stage(t):
        for h in (0, 1):
            mine = at.second_at(h)

            def turn(j, carry):
                got = dot(pick[h, j], p1[t, h, j]).astype(BF).reshape(2, SIDE, cap, half_w)
                st[t, h, :, :, j] = got
                return carry

            lax.fori_loop(0, SIDE, turn, 0)
            for s in (0, 1):
                own = st[t, h, s, pl.ds(mine, 1)].reshape(SIDE, cap, half_w)
                if h == 0:
                    xg[t, s, h, :, pl.ds(x, 1)] = own.reshape(SIDE, 1, cap, half_w)
                else:
                    xg[t, s, h, pl.ds(y, 1)] = own.reshape(1, SIDE, cap, half_w)

    def phase2(t, s):
        out = []
        for h in (0, 1):
            for k in steps:
                peer_at = lax.rem(at.second_at(h) + k, SIDE)
                dst = xg.at[t, s, h, :, x] if h == 0 else xg.at[t, s, h, y]
                out.append(
                    send(st.at[t, h, s, peer_at], dst, p2_s.at[t, s, h, k], p2_r.at[t, s, h, k], at.second(h, k))
                )
        return out

    moving = {}
    arrived(passing[0])
    stage(0)
    moving[0, 0] = phase2(0, 0)
    arrived(passing[1])
    stage(1)
    moving[1, 0] = phase2(1, 0)
    sent(passing[0] + passing[1])

    def slot_weights(n, carry):
        for s in (0, 1):
            q = rank[n, pl.ds(s * owners + me, 1), :]
            w = wt[n, pl.ds(s * owners + me, 1), :]
            col = jnp.sum(jnp.where(place == q, w, 0.0), axis=1, keepdims=True)
            row = (lax.rem(n, SIDE) * SIDE + n // SIDE) * cap
            wcol[s, pl.ds(pl.multiple_of(row, cap), cap), :] = jnp.broadcast_to(col, (cap, toks))
        return carry

    lax.fori_loop(0, SIDE * SIDE, slot_weights, 0)

    weights(wu_hbm, wu, n_chunks // 4, n_chunks)
    weights(wd_hbm, wd, 0, n_chunks)

    tile = 256
    h_tiles = hidden // tile
    d_tiles = 2 * half_w // tile
    per_half = half_w // tile

    def inputs(t, s, h):
        return xg[t, s, h].reshape(rows, half_w)

    def put(i, got, dst):
        cols = pl.ds(pl.multiple_of(lax.rem(i, per_half) * tile, tile), tile)
        dst[i // per_half, :, :, :, cols] = got.astype(BF).reshape(SIDE, SIDE, cap, tile)

    def forward(s):
        def turn(n, carry):
            cols = pl.ds(pl.multiple_of(n * tile, tile), tile)
            pre = dot(inputs(0, s, 0), wu[s, 0:half_w, cols]) + dot(inputs(0, s, 1), wu[s, half_w : 2 * half_w, cols])
            w = wcol[s, :, 0:1]
            sig = 1.0 / (1.0 + jnp.exp(-pre))
            right[1, s, :, cols] = (pre * sig * w).astype(BF)
            slope[s, :, cols] = sig * (1.0 + pre * (1.0 - sig)) * w
            return carry

        lax.fori_loop(0, h_tiles, turn, 0)
        sent(moving[0, s])

        def result(i, carry):
            put(i, dot(right[1, s], wd[s, pl.ds(pl.multiple_of(i * tile, tile), tile), :], 1, 1), st.at[0, :, s])
            return carry

        lax.fori_loop(0, d_tiles, result, 0)

    def core_copy(s, n):
        return pltpu.make_async_remote_copy(
            src_ref=xs.at[n % 2], dst_ref=cr.at[n], send_sem=c_s.at[s, n], recv_sem=c_r.at[s, n],
            device_id=at.other_core(), device_id_type=MESH,
        )

    def release_rows(t, s):
        for k in steps:
            for peer in (at.along_x(k), at.along_y(k)):
                pl.semaphore_signal(row_free.at[t, s], inc=1, device_id=peer, device_id_type=MESH)

    def gradient_tile(s, i, dst):
        cols = pl.ds(pl.multiple_of(lax.rem(i, per_half) * tile, tile), tile)

        def turn(t, carry):
            left = xg[t, s, i // per_half, :, :, :, cols].reshape(rows, tile)
            got = dot(left, right[t, s], 0, 0) * scale
            dst[:, pl.ds(pl.multiple_of(t * hidden, 128), hidden)] = got.astype(BF)
            return carry

        lax.fori_loop(0, 2, turn, 0)

    quarters = (2, 1, 3, 0)
    z_moving = {0: [], 1: []}

    def pair_sum(s, n):
        core_copy(s, n).wait_recv()
        step = quarters[n]
        zz = lax.rem(at.z + step, SIDE)
        own[s, zz] = (own[s, zz].astype(F32) + cr[n].astype(F32)).astype(BF)
        if step:
            z_moving[s].append(
                send(own.at[s, zz], zr.at[s, step - 1], z_s.at[s, step], z_r.at[s, step], at.along_z(step))
            )

    def backward(s):
        def turn(n, carry):
            cols = pl.ds(pl.multiple_of(n * tile, tile), tile)
            ga = dot(inputs(1, s, 0), wd[s, 0:half_w, cols]) + dot(inputs(1, s, 1), wd[s, half_w : 2 * half_w, cols])
            right[0, s, :, cols] = (ga * slope[s, :, cols]).astype(BF)
            return carry

        lax.fori_loop(0, h_tiles, turn, 0)
        if s:
            pl.semaphore_wait(core_free, 1)
        for n, step in enumerate(quarters):
            zz = lax.rem(at.z + step, SIDE)
            if n >= 2:
                core_copy(s, n - 2).wait_send()
            gradient_tile(s, zz * 2 + 1 - at.core, xs.at[n % 2])
            core_copy(s, n).start()
            gradient_tile(s, zz * 2 + at.core, own.at[s, zz])
            if n:
                pair_sum(s, n - 1)
        release_rows(1, s)

        def grad(i, carry):
            put(i, dot(right[0, s], wu[s, pl.ds(pl.multiple_of(i * tile, tile), tile), :], 1, 1), xg.at[1, s])
            return carry

        lax.fori_loop(0, d_tiles, grad, 0)
        pair_sum(s, 3)
        if s == 0:
            pl.semaphore_signal(core_free, inc=1, device_id=at.other_core(), device_id_type=MESH)
        for n in (2, 3):
            core_copy(s, n).wait_send()

    def result_rows(t, s, h, other):
        block = st.at[0, h, s] if t == 0 else xg.at[1, s, h]
        return block.at[:, other] if h == 0 else block.at[other]

    def home(t, s, h):
        return st.at[1, h, s] if t == 0 else xg.at[0, s, h]

    def return1(t, s):
        pl.semaphore_wait(row_free.at[t, s], 6)
        copies = []
        for h in (0, 1):
            mine = at.second_at(h)
            dst = home(t, s, h).at[mine]
            kept = pltpu.make_async_copy(result_rows(t, s, h, mine), dst, own_sem.at[t, s, h])
            kept.start()
            for k in steps:
                peer_at = lax.rem(mine + k, SIDE)
                copies.append(
                    send(result_rows(t, s, h, peer_at), dst, r1_s.at[t, s, h, k], r1_r.at[t, s, h, k], at.second(h, k))
                )
            copies.append(kept)
        return copies

    returning = {}
    arrived(moving[0, 0])
    moving[0, 1] = phase2(0, 1)
    forward(0)
    arrived(moving[1, 0])
    moving[1, 1] = phase2(1, 1)
    sent(moving[1, 0])
    release_rows(0, 0)
    backward(0)
    returning[0, 0] = return1(0, 0)
    returning[1, 0] = return1(1, 0)
    arrived(moving[0, 1])
    forward(1)
    arrived(moving[1, 1])
    sent(moving[1, 1])
    release_rows(0, 1)
    returning[0, 1] = return1(0, 1)
    backward(1)
    returning[1, 1] = return1(1, 1)

    last = {0: [], 1: []}
    homing = {0: [], 1: []}

    def return2(t):
        for h in (0, 1):
            for k in (2, 1, 3, 0):
                j = lax.rem(at.first_at(h) + k, SIDE)
                came = [home(t, s, h)[:, j].reshape(SIDE * cap, half_w) for s in (0, 1)]
                p1[t, h, k] = dot(pick[h, j], jnp.concatenate(came, axis=0), 0, 0).astype(BF)
                if k == 2:
                    for way, sem in ((1, 2), (3, 0)):
                        some = pl.ds((way // 2) * (toks // 2), toks // 2)
                        last[t].append(
                            send(
                                p1.at[t, h, 2, some], part.at[t, h, 1, some],
                                r2_s.at[t, h, sem], r2_r.at[t, h, sem], at.first(h, way),
                            )
                        )

    def return3(t):
        for c in last[t]:
            c.wait_recv()
        for h in (0, 1):
            for k in (1, 3):
                some = slice((k // 2) * (toks // 2), (k // 2 + 1) * (toks // 2))
                total = p1[t, h, k, some].astype(F32) + part[t, h, 1, some].astype(F32)
                p1[t, h, k, some] = total.astype(BF)
                homing[t].append(
                    send(p1.at[t, h, k], part.at[t, h, k - 1], r2_s.at[t, h, k], r2_r.at[t, h, k], at.first(h, k))
                )

    def finish(t):
        result = (out, ig)[t]
        for c in homing[t]:
            c.wait_recv()
        for h in (0, 1):
            total = p1[t, h, 0].astype(F32)
            for k in (1, 3):
                total = total + part[t, h, k - 1].astype(F32)
            result[:, h * half_w : (h + 1) * half_w] = total.astype(BF)

    def gradients(s, keep):
        room = (ld.at[0], ld.at[1], xs.at[0])
        copies = []
        for k in (1, 3, 2):
            z_moving[s][(2, 1, 3).index(k)].wait_recv()
            copy = pltpu.make_async_copy(zr.at[s, k - 1], room[k - 1], ld_sem.at[k - 1])
            copy.start()
            copies.append(copy)
        for copy in copies:
            copy.wait()

        def turn(r, carry):
            some = pl.ds(pl.multiple_of(r * 16, 16), 16)
            total = own[s, at.z, some].astype(F32)
            for buf in room:
                total = total + buf[some].astype(F32)
            keep(r, total.astype(BF))
            return carry

        lax.fori_loop(0, xs.shape[1] // 16, turn, 0)

    def exchange(number, src_of, dst_of, along):
        copies = []
        for u in (0, 1):
            use_x = along[u]
            mine = x if use_x else y
            kept = pltpu.make_async_copy(src_of(u, mine), dst_of(u, mine), mo_sem.at[number, u])
            kept.start()
            copies.append(kept)
            for k in steps:
                peer = at.along_x(k) if use_x else at.along_y(k)
                copies.append(
                    send(
                        src_of(u, lax.rem(mine + k, SIDE)), dst_of(u, mine),
                        m_s.at[number, u, k], m_r.at[number, u, k], peer,
                    )
                )
        return copies

    relocating = []

    def spread1():
        relocating.append(
            exchange(
                0, lambda u, o: fin.at[u, :, o] if u == 0 else fin.at[u, o], lambda u, m: ra.at[u, m], (True, False)
            )
        )

    def spread2():
        relocating.append(
            exchange(
                1,
                lambda u, o: ra.at[u, :, o],
                lambda u, m: rb.at[u, m] if u == 0 else rb.at[u, :, m],
                (False, True),
            )
        )

    def gather1():
        for i in range(SIDE * SIDE):
            for u in (0, 1):
                rd[u, i // SIDE, i % SIDE] = rb[u, partner[i] // SIDE, lax.rem(partner[i], SIDE)]
        relocating.append(
            exchange(
                2, lambda u, o: rd.at[u, o] if u == 0 else rd.at[u, :, o], lambda u, m: re.at[u, m], (False, True)
            )
        )

    def gather2():
        relocating.append(
            exchange(
                3,
                lambda u, o: re.at[u, :, o],
                lambda u, m: moved_up.at[:, m] if u == 0 else moved_down.at[m],
                (True, False),
            )
        )

    def keep_first(r, total):
        for u in (0, 1):
            fin[u, r // SIDE, lax.rem(r, SIDE)] = total[:, u * hidden : (u + 1) * hidden]

    def keep_second(r, total):
        xs[1, pl.ds(pl.multiple_of(r * 16, 16), 16)] = total

    gradients(0, keep_first)
    spread1()
    arrived(relocating[0])
    spread2()
    arrived(returning[0, 0])
    arrived(returning[0, 1])
    return2(0)
    arrived(relocating[1])
    gather1()
    return3(0)
    arrived(returning[1, 0])
    arrived(returning[1, 1])
    return2(1)
    arrived(relocating[2])
    gather2()
    return3(1)
    finish(0)
    gradients(1, keep_second)
    written = []
    for u, dst in enumerate((kept_up, kept_down)):
        copy = pltpu.make_async_copy(xs.at[1, :, pl.ds(u * hidden, hidden)], dst, g_sem.at[u])
        copy.start()
        written.append(copy)
    finish(1)
    arrived(relocating[3])
    for c in written:
        c.wait()
    sent(arriving[0] + arriving[1])
    for copies in list(returning.values()) + list(last.values()) + list(homing.values()) + list(z_moving.values()) + relocating:
        sent(copies)


def body(tokens, expert_ids, combine_weight, partner, w_up, w_down, out_grad):
    toks, chosen = expert_ids.shape
    width = tokens.shape[1]
    half_w = width // 2
    hidden = w_up.shape[2]
    owners = SIDE * SIDE
    cap = toks * chosen * 4 // (3 * 2 * owners)
    rows = owners * cap
    any_ = pl.BlockSpec(memory_space=pl.ANY)
    vmem = pl.BlockSpec(memory_space=pltpu.VMEM)
    n_rows = width // (2 * SIDE)
    piece = n_rows // owners
    tile_shape = jax.ShapeDtypeStruct((n_rows, hidden), BF)
    piece_shape = (SIDE, SIDE, piece, hidden)
    output, input_grad, moved_up, moved_down, kept_up, kept_down, *_ = pl.pallas_call(
        functools.partial(kernel, cap, chosen, 1.0 / toks),
        out_shape=(
            jax.ShapeDtypeStruct((toks, width), BF),
            jax.ShapeDtypeStruct((toks, width), BF),
            jax.ShapeDtypeStruct(piece_shape, BF),
            jax.ShapeDtypeStruct(piece_shape, BF),
            tile_shape,
            tile_shape,
            jax.ShapeDtypeStruct((2, SIDE - 1, n_rows, 2 * hidden), BF),
            jax.ShapeDtypeStruct((2, *piece_shape), BF),
            jax.ShapeDtypeStruct((2, *piece_shape), BF),
        ),
        in_specs=[pl.BlockSpec(memory_space=pltpu.SMEM), vmem, vmem, any_, any_, any_, any_],
        out_specs=(vmem, vmem, any_, any_, any_, any_, any_, any_, any_),
        scratch_shapes=[
            pltpu.VMEM((owners, 16, toks), F32),
            pltpu.VMEM((owners, 2 * owners, toks), F32),
            pltpu.VMEM((owners, 2 * owners, toks), F32),
            pltpu.VMEM((2, SIDE, 2 * SIDE * cap, toks), BF),
            pltpu.VMEM((2, 2, SIDE, toks, half_w), BF),
            pltpu.VMEM((2, 2, 2, SIDE, SIDE, cap, half_w), BF),
            pltpu.VMEM((2, 2, 2, SIDE, SIDE, cap, half_w), BF),
            pltpu.VMEM((2, width, hidden), BF),
            pltpu.VMEM((2, width, hidden), BF),
            pltpu.VMEM((2, 128, 2, hidden), BF),
            pltpu.VMEM((2, rows, toks), F32),
            pltpu.VMEM((2, rows, hidden), F32),
            pltpu.VMEM((2, 2, rows, hidden), BF),
            pltpu.VMEM((2, 2, SIDE - 1, toks, half_w), BF),
            pltpu.VMEM((2, SIDE, n_rows, 2 * hidden), BF),
            pltpu.VMEM((2, n_rows, 2 * hidden), BF),
            pltpu.VMEM((2, n_rows, 2 * hidden), BF),
            pltpu.VMEM((SIDE, n_rows, 2 * hidden), BF),
            pltpu.VMEM((2, *piece_shape), BF),
            pltpu.VMEM((2, *piece_shape), BF),
            pltpu.VMEM((2, *piece_shape), BF),
            DMA((2, 4)), DMA((2, 4)),
            DMA((2, 2, 4)), DMA((2, 2, 4)), DMA((2, 2)),
            DMA((2, 2, 2, 4)), DMA((2, 2, 2, 4)),
            DMA((2,)),
            DMA((2, 2, 2, 4)), DMA((2, 2, 2, 4)), DMA((2, 2, 2)),
            DMA((2, 2, 4)), DMA((2, 2, 4)),
            DMA((2, 4)), DMA((2, 4)), DMA((2, 4)), DMA((2, 4)), DMA((3,)), DMA((2,)),
            DMA((4, 2, 4)), DMA((4, 2, 4)), DMA((4, 2)),
            pltpu.SemaphoreType.REGULAR((2, 2)), pltpu.SemaphoreType.REGULAR,
        ],
        compiler_params=pltpu.CompilerParams(
            collective_id=0, has_side_effects=True, vmem_limit_bytes=62 << 20
        ),
    )(partner, expert_ids.T, combine_weight.T, tokens, out_grad, w_up, w_down)

    grad_up = jnp.stack([moved_up.reshape(n_rows, hidden), kept_up], axis=1)
    grad_down = jnp.stack([moved_down.reshape(n_rows, hidden), kept_down], axis=1)
    return (output, input_grad, grad_up, grad_down)


def solution(mesh):
    return jax.shard_map(
        body,
        mesh=mesh,
        in_specs=(
            P(("dp", "expert"), None),
            P(("dp", "expert"), None),
            P(("dp", "expert"), None),
            P(),
            P(None, "expert", None),
            P(None, "expert", None),
            P(("dp", "expert"), None),
        ),
        out_specs=(
            P(("dp", "expert"), None),
            P(("dp", "expert"), None),
            P("dp", "expert", None),
            P("dp", "expert", None),
        ),
        check_vma=False,
    )
```
